512 devices in a mesh: dp: 32 (over x_hi, z, core), tensor: 16 (over x_lo, y).
Axes of the slice: x: 4 (x_hi: 2, x_lo: 2; x = x_hi * 2 + x_lo), y: 8, z: 8, core: 2. Of those that a mesh axis runs over, the one named last changes fastest.
Arguments:
- hidden_in: bfloat16 [7680, 4, 5120], P('dp', None, 'tensor'), may hold values from -6 to 6
- kv_weight: bfloat16 [2, 5120, 1024], P(None, 'tensor'), may hold values from -0.078125 to 0.078125
- factor_a: float32 [2, 64, 5120], P(None, None, 'tensor'), may hold values from -0.078125 to 0.078125
- factor_b: float32 [2, 64, 1024], P(None, None, 'tensor'), may hold values from -0.75 to 0.75
- grad_a: float32 [32, 2, 64, 5120], P('dp', None, None, 'tensor'), may hold values from -6 to 6
- grad_b: float32 [32, 2, 64, 1024], P('dp', None, None, 'tensor'), may hold values from -6 to 6
- key_gain: float32 [128], replicated, may hold values from 0.1 to 1.9
- queries: bfloat16 [7680, 4, 4096], P(('dp', 'tensor')), may hold values from -27 to 27
- cache_keys: bfloat16 [7680, 16, 1024], P(('dp', 'tensor')), may hold values from -6 to 6
- cache_values: bfloat16 [7680, 16, 1024], P(('dp', 'tensor')), may hold values from -6 to 6
- cache_lengths: int32 [7680], P(('dp', 'tensor')), may hold values from 2 to 12, as said below
- positions: int32 [7680], P(('dp', 'tensor')), may hold values from 0 to 32767
Outputs:
- attended: bfloat16 [7680, 4, 4096], P(('dp', 'tensor'))
- new_a: float32 [2, 64, 5120], P(None, None, 'tensor')
- new_b: float32 [2, 64, 1024], P(None, None, 'tensor')
The draws below stay inside these ranges and needn't reach their ends.
Inputs may be any that keep to these rules, and one draw needn't show every extreme that they name: `cache_lengths`: some row holds 12 filled slots.
All inputs are finite; a program needn't handle non-finite values.
Results may differ from the reference program's by a relative error of at most 0.035.
Values may be sent and summed in bfloat16 or wider, within the bound.
A program may use at most 64 MiB of HBM per device.

```python
import math
import jax
import jax.numpy as jnp
from jax import lax

D = 5120
KVH = 8
HD = 128
QH = 32
R = 64
STEPS = 4
CACHE = 16
KVW = 1024
ROWS = 7680
N_DP = 32
N_TENSOR = 16


def draw_cache_keys(key, part):
    key = jax.random.fold_in(key, 21)
    keys = jnp.clip(jax.random.normal(key, (ROWS, CACHE, KVH, HD), jnp.float32), -6.0, 6.0)
    return keys.reshape(ROWS, CACHE, KVH * HD).astype(jnp.bfloat16)


def draw_queries(key, part):
    key = jax.random.fold_in(key, 22)
    values = jnp.clip(jax.random.normal(key, (ROWS, STEPS, QH * HD), jnp.float32), -6.0, 6.0)
    return values.astype(jnp.bfloat16)


def draw_cache_lengths(key, part):
    key = jax.random.fold_in(key, 23)
    first, second = jax.random.split(key)
    lengths = jax.random.randint(first, (ROWS,), 2, CACHE - STEPS + 1)
    full_row = jax.random.randint(second, (), 0, ROWS)
    return jnp.where(jnp.arange(ROWS) == full_row, CACHE - STEPS, lengths).astype(jnp.int32)


def with_ends(entries, own_key, least, largest):
    spot = [jax.random.randint(jax.random.fold_in(own_key, axis), (), 0, length) for axis, length in enumerate(entries.shape)]
    widest = entries.shape.index(max(entries.shape))
    next_to = spot[:widest] + [(spot[widest] + 1) % entries.shape[widest]] + spot[widest + 1:]
    return entries.at[tuple(spot)].set(least).at[tuple(next_to)].set(largest)


def steps_of(stream_key, extent, shards, least, top_value):
    factor_of = 1.0
    for dim, parts in shards:
        steps = jax.random.uniform(jax.random.fold_in(jax.random.fold_in(stream_key, 6), dim), (parts,), jnp.float32, least / len(shards), top_value / len(shards))
        factor_of = factor_of * jnp.repeat(jnp.exp(steps), extent[dim] // parts).reshape((-1,) + (1,) * (len(extent) - 1 - dim))
    return factor_of


def bell_draw(key, extent, scale, most, cuts=(), kind=jnp.bfloat16):
    factor_of = steps_of(key, extent, cuts, -0.22, 0.18) if cuts else 1.0
    drawn = jax.random.normal(key, extent, jnp.float32) * scale * factor_of
    return jnp.minimum(jnp.maximum(drawn, -most), most).astype(kind)


def setup_inputs(seed: int = 0) -> dict:
    key_list = jax.random.split(jax.random.key(seed), 13)
    hidden_in = bell_draw(key_list[0], (ROWS, STEPS, D), 1.0, 6.0, ((0, 32), (2, 16)))
    kv_weight = bell_draw(key_list[1], (2, D, KVW), D ** -0.5, 0.078125, ((1, 16),))
    factor_a = bell_draw(key_list[2], (2, R, D), D ** -0.5, 0.078125, ((2, 16),), jnp.float32)
    factor_b = bell_draw(key_list[3], (2, R, KVW), R ** -0.5, 0.75, ((2, 16),), jnp.float32)
    grad_a = bell_draw(key_list[4], (N_DP, 2, R, D), 1.0, 6.0, ((0, 32), (3, 16)), jnp.float32)
    grad_b = bell_draw(key_list[5], (N_DP, 2, R, KVW), 1.0, 6.0, ((0, 32), (3, 16)), jnp.float32)
    key_gain = jnp.clip(1.0 + 0.18 * jax.random.normal(key_list[6], (HD,), jnp.float32), 0.1, 1.9)
    queries = draw_queries(jax.random.fold_in(key_list[12], 71), 0)
    cache_keys = draw_cache_keys(jax.random.fold_in(key_list[12], 71), 0)
    cache_values = bell_draw(key_list[9], (ROWS, CACHE, KVW), 1.0, 6.0, ((0, 512),))
    cache_lengths = draw_cache_lengths(jax.random.fold_in(key_list[12], 71), 0)
    positions = with_ends(jax.random.randint(key_list[11], (ROWS,), 0, 32768), jax.random.fold_in(key_list[11], 1), 0, 32767).astype(jnp.int32)
    return {"hidden_in": hidden_in, "kv_weight": kv_weight, "factor_a": factor_a, "factor_b": factor_b, "grad_a": grad_a, "grad_b": grad_b, "key_gain": key_gain, "queries": queries, "cache_keys": cache_keys, "cache_values": cache_values, "cache_lengths": cache_lengths, "positions": positions}


def normed_rotated(keys, gain, position):
    scale = lax.rsqrt(lax.optimization_barrier(jnp.mean(keys * keys, axis=-1, keepdims=True)) + 1e-06)
    keys = keys * scale * gain
    half = keys.shape[-1] // 2
    freq = jnp.exp(-math.log(1000000.0) * (jnp.arange(half, dtype=jnp.float32) * 2.0 / keys.shape[-1]))
    angle = position.astype(jnp.float32)[..., None] * freq
    cosine = jnp.concatenate([jnp.cos(angle), jnp.cos(angle)], axis=-1)[..., None, :]
    sine = jnp.concatenate([jnp.sin(angle), jnp.sin(angle)], axis=-1)[..., None, :]
    turned = jnp.concatenate([-keys[..., half:], keys[..., :half]], axis=-1)
    return keys * cosine + turned * sine

def attend(queries, cache_keys, cache_values, new_keys, new_values, lengths):
    rows, steps, width = queries.shape
    slots = cache_keys.shape[1]
    slot = jnp.arange(slots, dtype=jnp.int32)
    for step in range(steps):
        hit = (slot[None, :] == lengths[:, None] + step)[:, :, None]
        cache_keys = jnp.where(hit, new_keys[:, step][:, None, :], cache_keys)
        cache_values = jnp.where(hit, new_values[:, step][:, None, :], cache_values)
    groups = QH // KVH
    query_five = queries.reshape(rows, steps, KVH, groups, HD).astype(jnp.float32)
    key_four = cache_keys.reshape(rows, slots, KVH, HD).astype(jnp.float32)
    value_four = cache_values.reshape(rows, slots, KVH, HD).astype(jnp.float32)
    scores = jnp.einsum('rtkgd,rckd->rtkgc', query_five, key_four) * HD ** (-0.5)
    limit = lengths[:, None] + jnp.arange(steps, dtype=jnp.int32)[None, :]
    valid = (slot[None, None, :] <= limit[:, :, None])[:, :, None, None, :]
    scores = jnp.where(valid, scores, jnp.float32(-1e+30))
    top = lax.optimization_barrier(jnp.max(scores, axis=-1, keepdims=True))
    expo = jnp.exp(scores - top)
    weights = (expo / lax.optimization_barrier(jnp.sum(expo, axis=-1, keepdims=True))).astype(jnp.bfloat16)
    result = jnp.einsum('rtkgc,rckd->rtkgd', weights.astype(jnp.float32), value_four)
    return result.reshape(rows, steps, width).astype(jnp.bfloat16)

def reference(hidden_in, kv_weight, factor_a, factor_b, grad_a, grad_b, key_gain, queries, cache_keys, cache_values, cache_lengths, positions):
    new_a = factor_a - 2.0 / math.sqrt(N_DP * D) * lax.optimization_barrier(jnp.sum(grad_a, axis=0))
    new_b = factor_b - 2.0 / math.sqrt(N_DP * R) * lax.optimization_barrier(jnp.sum(grad_b, axis=0))
    delta = jnp.einsum('prd,prk->pdk', new_a, new_b, precision=lax.Precision.HIGHEST)
    merged = (kv_weight.astype(jnp.float32) + 0.25 * delta).astype(jnp.bfloat16)
    joined = jnp.concatenate([merged[0], merged[1]], axis=1)
    block = D // N_TENSOR
    flat = hidden_in.reshape(ROWS * STEPS, D)

    def shard_sum(total, index):
        part_x = lax.dynamic_slice_in_dim(flat, index * block, block, 1)
        part_w = lax.dynamic_slice_in_dim(joined, index * block, block, 0)
        term = jnp.dot(part_x, part_w, preferred_element_type=jnp.float32).astype(jnp.bfloat16)
        return (total + term.astype(jnp.float32), None)
    start_total = jnp.zeros((ROWS * STEPS, 2 * KVW), jnp.float32)
    projected, _ = lax.scan(shard_sum, start_total, jnp.arange(N_TENSOR, dtype=jnp.int32))
    projected = projected.reshape(ROWS, STEPS, 2 * KVW)
    place = positions[:, None] + jnp.arange(STEPS, dtype=jnp.int32)[None, :]
    keys = normed_rotated(projected[..., :KVW].reshape(ROWS, STEPS, KVH, HD), key_gain, place)
    new_keys = keys.reshape(ROWS, STEPS, KVW).astype(jnp.bfloat16)
    new_values = projected[..., KVW:].astype(jnp.bfloat16)
    attended = attend(queries, cache_keys, cache_values, new_keys, new_values, cache_lengths)
    return (attended, new_a, new_b)
```

```python
import math

import jax
import jax.numpy as jnp
from jax import lax
from jax.experimental import pallas as pl
from jax.experimental.pallas import tpu as pltpu
from jax.sharding import PartitionSpec as P

D = 5120
KVH = 8
HD = 128
QH = 32
R = 64
STEPS = 4
KV = 2048
MESH = pl.DeviceIdType.MESH

NY = 8
NZ = 8
TOK = 64
DS = 320
NC = 4
CW = 512
HALF = CW // 2
ORDER = (4, 3, 5, 2, 6, 1, 7, 0)
GR = 384
GH = GR // 2
GZ = GH // NZ
F32 = jnp.float32
BF = jnp.bfloat16


def transfer_kernel(
    rate_a, rate_b,
    hb, kv, ga, gb, fa, fb,
    proj, na, nb,
    hown, hrem, wown, wrem, pk,
    sb0, rb0, sb, rb, pu, sbu, rbu,
    tpad, gT, g1s, g1r, g2s, g2r, h2, g3r, tot, naown, narem, nbt, nball,
    loc, ssem, rsem,
):
    dp = lax.axis_index("dp")
    tn = lax.axis_index("tensor")
    xh, z, c = dp // 16, lax.rem(dp // 2, 8), lax.rem(dp, 2)
    a, y = tn // NY, lax.rem(tn, NY)
    dsib = dp + 1 - 2 * c
    dflip = lax.rem(dp + 16, 32)
    tflip = lax.rem(tn + 8, 16)
    sib = (dsib, tn)
    xflip = (dflip, tn)
    part = (dp, tflip)
    other = (dflip, tflip)
    partsib = (dsib, tflip)
    up = (dp, a * NY + lax.rem(y + 1, NY))
    down = (dp, a * NY + lax.rem(y + NY - 1, NY))
    zpeer = [None] + [(xh * 16 + lax.rem(z + i, NZ) * 2 + c, tn) for i in range(1, NZ)]
    ring = (up, down)
    peers = [sib, xflip, part, other, partsib, up, down] + zpeer[1:]

    barrier = pltpu.get_barrier_semaphore()
    for peer in peers:
        pl.semaphore_signal(barrier, inc=1, device_id=peer, device_id_type=MESH)

    def block(side, j):
        row = (side * NY + lax.rem(y + j, NY)) * TOK
        return hb.at[pl.ds(pl.multiple_of(row, TOK), TOK)]

    lh = []
    for i, j in enumerate(ORDER):
        cp = pltpu.make_async_copy(block(a, j), hown.at[pl.ds(i * TOK, TOK)], loc.at[i])
        cp.start()
        lh.append(cp)
    lw = []
    for k in range(NC):
        cols = pl.ds((k % 2) * CW, CW)
        cp = pltpu.make_async_copy(kv.at[k // 2, :, cols], wown.at[k // 2, :, cols], loc.at[8 + k])
        cp.start()
        lw.append(cp)

    count = [0]
    started = []

    def remote(src, dst, device):
        i = count[0]
        count[0] += 1
        cp = pltpu.make_async_remote_copy(
            src_ref=src, dst_ref=dst, send_sem=ssem.at[i], recv_sem=rsem.at[i],
            device_id=device, device_id_type=MESH,
        )
        cp.start()
        started.append(cp)
        return cp

    tpad[...] = jnp.zeros_like(tpad)
    tpad[:, 0:DS] = ga[...]
    gT[...] = tpad[...].T
    tpad[:, 0:R] = gb[...]
    gT[DS:GR, :] = tpad[:, 0:128].T[0:R, :]

    pl.semaphore_wait(barrier, len(peers))

    krow = c * (DS // 2)

    def weight(k, lo, n, device):
        rows = pl.ds(pl.multiple_of(krow + lo, 16), n)
        cols = pl.ds((k % 2) * CW, CW)
        return remote(kv.at[k // 2, rows, cols], wrem.at[k // 2, rows, cols], device)

    def forward(k):
        rows = pl.ds(pl.multiple_of(krow, 16), DS // 2)
        cols = pl.ds((k % 2) * CW, CW)
        ref = wrem.at[k // 2, rows, cols]
        return remote(ref, ref, sib)

    def hidden(i):
        return remote(block(1 - a, ORDER[i]), hrem.at[pl.ds(i * TOK, TOK)], part)

    w0a = weight(0, 0, 80, part)
    w0b = weight(0, 80, 80, other)
    mine = pl.multiple_of(c * GH, GH)
    theirs = pl.multiple_of((1 - c) * GH, GH)
    g1s[...] = gT[pl.ds(theirs, GH), :].astype(BF)
    g1 = remote(g1s, g1r, sib)
    hr = [hidden(i) for i in range(5)]
    w1 = weight(1, 0, 160, other)
    hr += [hidden(i) for i in range(5, 8)]
    w2 = weight(2, 0, 160, other)
    w3 = weight(3, 0, 160, part)

    def product(k, lo, n):
        cols = slice((k % 2) * CW, (k % 2) * CW + CW)
        pk[k, lo:lo + n, :] = jnp.dot(
            hown[lo:lo + n, :], wown[k // 2, :, cols], preferred_element_type=F32
        ) + jnp.dot(hrem[lo:lo + n, :], wrem[k // 2, :, cols], preferred_element_type=F32)

    sent = {}

    def stage(k, s):
        if s == 0:
            for way in range(2):
                cut = slice(way * HALF, way * HALF + HALF)
                sb0[k, way] = pk[k, 0:TOK, cut].astype(BF)
                sent[k, 0, way] = remote(sb0.at[k, way], rb0.at[k, way], ring[way])
            return
        for way in range(2):
            lo = (2 * s - 1 + way) * TOK
            sent[k, s - 1, way].wait_recv()
            if s == 1:
                cut = slice(way * HALF, way * HALF + HALF)
                rest = slice((1 - way) * HALF, (1 - way) * HALF + HALF)
                sb[k, 0, way, :, cut] = (
                    pk[k, lo:lo + TOK, cut] + rb0[k, way].astype(F32)
                ).astype(BF)
                sb[k, 0, way, :, rest] = pk[k, lo:lo + TOK, rest].astype(BF)
            else:
                sb[k, s - 1, way] = (
                    pk[k, lo:lo + TOK, :] + rb[k, s - 2, way].astype(F32)
                ).astype(BF)
            sent[k, s, way] = remote(sb.at[k, s - 1, way], rb.at[k, s - 1, way], ring[way])

    def last(k):
        for way in range(2):
            sent[k, 3, way].wait_recv()
        proj[:, k * CW:(k + 1) * CW] = (
            pk[k, 7 * TOK:, :] + rb[k, 2, 0].astype(F32) + rb[k, 2, 1].astype(F32)
        )

    usent = {}

    def ustage(s):
        if s == 0:
            sbu[0, 0] = pu[0:TOK, :].astype(BF)
            usent[0, 0] = remote(sbu.at[0, 0], rbu.at[0, 0], up)
            return
        for way in range(2):
            lo = (2 * s - 1 + way) * TOK
            total = pu[lo:lo + TOK, :]
            if s > 1 or way == 0:
                usent[s - 1, way].wait_recv()
                total = total + rbu[s - 1, way].astype(F32)
            sbu[s, way] = total.astype(BF)
            usent[s, way] = remote(sbu.at[s, way], rbu.at[s, way], ring[way])

    bsent = {}
    bcols = pl.ds(pl.multiple_of(c * 32, 32), 32)

    def bstage(s):
        if s > 0:
            bsent[s - 1, 0].wait_recv()
            if s < 3:
                bsent[s - 1, 1].wait_recv()
        for way in range(2 if s < 3 else 1):
            from_y = lax.rem(y + NY - s, NY) if way == 0 else lax.rem(y + s, NY)
            ref = nball.at[a * NY + from_y, bcols, :]
            bsent[s, way] = remote(ref, ref, ring[way])

    w0a.wait_recv()
    w0b.wait_recv()
    f0 = forward(0)
    g1.wait_recv()
    g2s[...] = (gT[pl.ds(mine, GH), :] + g1r[...].astype(F32)).astype(BF)
    g2 = remote(g2s, g2r, xflip)
    lw[0].wait()
    lh[0].wait()
    hr[0].wait_recv()
    f0.wait_recv()
    product(0, 0, TOK)
    stage(0, 0)
    for i in (1, 2):
        lh[i].wait()
        hr[i].wait_recv()
    product(0, TOK, 2 * TOK)

    stage(0, 1)
    g2.wait_recv()
    h2[...] = g2s[...].astype(F32) + g2r[...].astype(F32)
    g3 = []
    for i in range(1, NZ):
        rows = pl.ds(pl.multiple_of(lax.rem(z + i, NZ) * GZ, GZ), GZ)
        g3.append(remote(h2.at[rows, :], g3r.at[i], zpeer[i]))
    w1.wait_recv()
    f1 = forward(1)
    for i in range(3, 8):
        lh[i].wait()
        hr[i].wait_recv()
    product(0, 3 * TOK, 5 * TOK)
    lw[1].wait()
    f1.wait_recv()
    product(1, 0, 8 * TOK)
    stage(1, 0)

    stage(0, 2)
    stage(1, 1)
    total = h2[pl.ds(pl.multiple_of(z * GZ, GZ), GZ), :]
    for i in range(1, NZ):
        g3[i - 1].wait_recv()
        total = total + g3r[i]
    piece = pl.ds(pl.multiple_of(c * GH + z * GZ, GZ), GZ)
    tot[piece, :] = total
    g4 = [remote(tot.at[piece, :], tot.at[piece, :], zpeer[i]) for i in range(1, NZ)]
    w2.wait_recv()
    f2 = forward(2)
    lw[2].wait()
    f2.wait_recv()
    product(2, 0, 8 * TOK)
    stage(2, 0)

    stage(0, 3)
    stage(1, 2)
    stage(2, 1)
    for cp in g4:
        cp.wait_recv()
    half = tot.at[pl.ds(mine, GH), :]
    g5 = remote(half, half, sib)
    w3.wait_recv()
    f3 = forward(3)
    lw[3].wait()
    f3.wait_recv()
    product(3, 0, 8 * TOK)
    stage(3, 0)
    tpad[:, 0:DS] = fa[...]
    faT = tpad[...].T[0:DS, :]
    tpad[:, 0:R] = fb[...]
    fbT = tpad[:, 0:128].T[0:R, :]
    g5.wait_recv()
    naown[...] = (faT - rate_a * tot[0:DS, :]).astype(BF)
    n1 = remote(naown, narem, part)
    nbt[...] = fbT - rate_b * tot[DS:GR, :]
    nball[tn, bcols, :] = nbt[bcols, :].astype(BF)
    bstage(0)

    last(0)
    stage(1, 3)
    stage(2, 2)
    stage(3, 1)
    n1.wait_recv()
    pu[...] = jnp.dot(hown[...], naown[...], preferred_element_type=F32) + jnp.dot(
        hrem[...], narem[...], preferred_element_type=F32
    )
    ustage(0)
    bstage(1)
    back = tot[...].T
    na[...] = fa[...] - rate_a * back[:, 0:DS]
    nb[...] = fb[...] - rate_b * back[:, DS:GR]

    last(1)
    stage(2, 3)
    stage(3, 2)
    bstage(2)
    ustage(1)

    last(2)
    stage(3, 3)
    ustage(2)
    bstage(3)
    ustage(3)

    bsent[3, 0].wait_recv()
    bsent[2, 1].wait_recv()
    mineb = nball.at[pl.ds(pl.multiple_of(a * NY, NY), NY), bcols, :]
    shared = [remote(mineb, mineb, device) for device in (sib, part, partsib)]
    last(3)
    for way in range(2):
        usent[3, way].wait_recv()
    u = (pu[7 * TOK:, :] + rbu[3, 0].astype(F32) + rbu[3, 1].astype(F32)) * 0.25
    lane = lax.broadcasted_iota(jnp.int32, u.shape, 1)
    for cp in shared:
        cp.wait_recv()
    allb = nball[...].reshape(16 * R, 128)
    for p in range(2):
        up_ = jnp.where((lane >= p * R) & (lane < p * R + R), u, 0.0).astype(BF)
        proj[:, p * 1024:(p + 1) * 1024] += lax.dot_general(
            up_, allb, (((1,), (1,)), ((), ())), preferred_element_type=F32
        )
    for cp in started:
        cp.wait_send()


N_REMOTE = 5 + 4 + 8 + 32 + 7 + 2 + 7 + 7 + 1 + 1 + 7 + 3


def transfers(rate_a, rate_b, hb, kv, ga, gb, fa, fb):
    def body(*refs):
        transfer_kernel(rate_a, rate_b, *refs)

    vmem = pl.BlockSpec(memory_space=pltpu.VMEM)
    hbm = pl.BlockSpec(memory_space=pl.ANY)
    return pl.pallas_call(
        body,
        out_shape=(
            jax.ShapeDtypeStruct((TOK, KV), F32),
            jax.ShapeDtypeStruct((2 * R, DS), F32),
            jax.ShapeDtypeStruct((2 * R, R), F32),
        ),
        in_specs=[hbm, hbm, vmem, vmem, vmem, vmem],
        out_specs=(vmem, vmem, vmem),
        scratch_shapes=[
            pltpu.VMEM((8 * TOK, DS), BF),
            pltpu.VMEM((8 * TOK, DS), BF),
            pltpu.VMEM((2, DS, 1024), BF),
            pltpu.VMEM((2, DS, 1024), BF),
            pltpu.VMEM((NC, 8 * TOK, CW), F32),
            pltpu.VMEM((NC, 2, TOK, HALF), BF),
            pltpu.VMEM((NC, 2, TOK, HALF), BF),
            pltpu.VMEM((NC, 3, 2, TOK, CW), BF),
            pltpu.VMEM((NC, 3, 2, TOK, CW), BF),
            pltpu.VMEM((8 * TOK, 128), F32),
            pltpu.VMEM((4, 2, TOK, 128), BF),
            pltpu.VMEM((4, 2, TOK, 128), BF),
            pltpu.VMEM((128, GR), F32),
            pltpu.VMEM((GR, 128), F32),
            pltpu.VMEM((GH, 128), BF),
            pltpu.VMEM((GH, 128), BF),
            pltpu.VMEM((GH, 128), BF),
            pltpu.VMEM((GH, 128), BF),
            pltpu.VMEM((GH, 128), F32),
            pltpu.VMEM((NZ, GZ, 128), F32),
            pltpu.VMEM((GR, 128), F32),
            pltpu.VMEM((DS, 128), BF),
            pltpu.VMEM((DS, 128), BF),
            pltpu.VMEM((R, 128), F32),
            pltpu.VMEM((16, R, 128), BF),
            pltpu.SemaphoreType.DMA((12,)),
            pltpu.SemaphoreType.DMA((N_REMOTE,)),
            pltpu.SemaphoreType.DMA((N_REMOTE,)),
        ],
        compiler_params=pltpu.CompilerParams(
            collective_id=0, has_side_effects=True, vmem_limit_bytes=48 * 1024 * 1024
        ),
    )(hb, kv, ga, gb, fa, fb)


def normed_rotated(keys, gain, position):
    scale = lax.rsqrt(jnp.mean(keys * keys, axis=-1, keepdims=True) + 1e-06)
    keys = keys * scale * gain
    half = keys.shape[-1] // 2
    freq = jnp.exp(
        -math.log(1000000.0) * (jnp.arange(half, dtype=jnp.float32) * 2.0 / keys.shape[-1])
    )
    angle = position.astype(jnp.float32)[..., None] * freq
    cosine = jnp.concatenate([jnp.cos(angle), jnp.cos(angle)], axis=-1)[..., None, :]
    sine = jnp.concatenate([jnp.sin(angle), jnp.sin(angle)], axis=-1)[..., None, :]
    turned = jnp.concatenate([-keys[..., half:], keys[..., :half]], axis=-1)
    return keys * cosine + turned * sine


def attend(queries, cache_keys, cache_values, new_keys, new_values, lengths):
    rows, steps, width = queries.shape
    slots = cache_keys.shape[1]
    slot = jnp.arange(slots, dtype=jnp.int32)
    for step in range(steps):
        hit = (slot[None, :] == lengths[:, None] + step)[:, :, None]
        cache_keys = jnp.where(hit, new_keys[:, step][:, None, :], cache_keys)
        cache_values = jnp.where(hit, new_values[:, step][:, None, :], cache_values)
    groups = QH // KVH
    query_five = queries.reshape(rows, steps, KVH, groups, HD)
    key_four = cache_keys.reshape(rows, slots, KVH, HD)
    value_four = cache_values.reshape(rows, slots, KVH, HD)
    scores = jnp.einsum(
        "rtkgd,rckd->rtkgc", query_five, key_four, preferred_element_type=jnp.float32
    ) * HD ** (-0.5)
    limit = lengths[:, None] + jnp.arange(steps, dtype=jnp.int32)[None, :]
    valid = (slot[None, None, :] <= limit[:, :, None])[:, :, None, None, :]
    scores = jnp.where(valid, scores, jnp.float32(-1e30))
    top = jnp.max(scores, axis=-1, keepdims=True)
    expo = jnp.exp(scores - top)
    weights = (expo / jnp.sum(expo, axis=-1, keepdims=True)).astype(jnp.bfloat16)
    result = jnp.einsum(
        "rtkgc,rckd->rtkgd", weights, value_four, preferred_element_type=jnp.float32
    )
    return result.reshape(rows, steps, width).astype(jnp.bfloat16)


def per_device(
    hidden_in, kv_weight, factor_a, factor_b, grad_a, grad_b, key_gain,
    queries, cache_keys, cache_values, cache_lengths, positions,
):
    groups_dp = lax.axis_size("dp")
    rate_a = 2.0 / math.sqrt(groups_dp * D)
    rate_b = 2.0 / math.sqrt(groups_dp * R)
    rows_here = queries.shape[0]
    hb = jnp.pad(hidden_in.reshape(16, rows_here * STEPS, DS), ((0, 0), (0, 4), (0, 0)))
    proj, na, nb = transfers(
        rate_a, rate_b, hb.reshape(16 * TOK, DS), kv_weight,
        grad_a.reshape(2 * R, DS), grad_b.reshape(2 * R, R),
        factor_a.reshape(2 * R, DS), factor_b.reshape(2 * R, R),
    )
    new_a = na.reshape(2, R, DS)
    new_b = nb.reshape(2, R, R)
    projected = proj[:rows_here * STEPS].reshape(rows_here, STEPS, KV)
    kv_width = KVH * HD
    place = positions[:, None] + jnp.arange(STEPS, dtype=jnp.int32)[None, :]
    keys = normed_rotated(
        projected[..., :kv_width].reshape(rows_here, STEPS, KVH, HD), key_gain, place
    )
    new_keys = keys.reshape(rows_here, STEPS, kv_width).astype(jnp.bfloat16)
    new_values = projected[..., kv_width:].astype(jnp.bfloat16)
    attended = attend(queries, cache_keys, cache_values, new_keys, new_values, cache_lengths)
    return (attended, new_a, new_b)


def solution(mesh):
    return jax.shard_map(
        per_device,
        mesh=mesh,
        in_specs=(
            P("dp", None, "tensor"),
            P(None, "tensor", None),
            P(None, None, "tensor"),
            P(None, None, "tensor"),
            P("dp", None, None, "tensor"),
            P("dp", None, None, "tensor"),
            P(),
            P(("dp", "tensor"), None, None),
            P(("dp", "tensor"), None, None),
            P(("dp", "tensor"), None, None),
            P(("dp", "tensor")),
            P(("dp", "tensor")),
        ),
        out_specs=(
            P(("dp", "tensor"), None, None),
            P(None, None, "tensor"),
            P(None, None, "tensor"),
        ),
        check_vma=False,
    )
```

```python
import math

import jax
import jax.numpy as jnp
from jax import lax
from jax.experimental import pallas as pl
from jax.experimental.pallas import tpu as pltpu
from jax.sharding import PartitionSpec as P

D = 5120
KVH = 8
HD = 128
QH = 32
R = 64
STEPS = 4
KV = 2048
MESH = pl.DeviceIdType.MESH

NY = 8
NZ = 8
TOK = 64
DS = 320
NC = 4
CW = 512
HALF = CW // 2
ORDER = (4, 3, 5, 2, 6, 1, 7, 0)
GR = 384
GH = GR // 2
GZ = GH // NZ
ROWS = 15
SCALE = HD ** -0.5
NEG = -1e30
F32 = jnp.float32
BF = jnp.bfloat16


def transfer_kernel(
    rate_a, rate_b,
    hT, kv, ga, gb, fa, fb, gain, q, ck, cv, lens, pos,
    out, na, nb,
    hin, hsend, hown, hrem, wown, wrem, pk,
    sb0, rb0, sb, rb, pu, sbu, rbu,
    tpad, gT, fT, g1s, g1r, g2s, g2r, h2, g3r, tot, full, nball,
    qin, qs, qh, kc, vc, biasc, biasn, cost, sint, mc, lc, oc, pn, of,
    loc, ssem, rsem,
):
    dp = lax.axis_index("dp")
    tn = lax.axis_index("tensor")
    xh, z, c = dp // 16, lax.rem(dp // 2, 8), lax.rem(dp, 2)
    a, y = tn // NY, lax.rem(tn, NY)
    dsib = dp + 1 - 2 * c
    dflip = lax.rem(dp + 16, 32)
    tflip = lax.rem(tn + 8, 16)
    sib = (dsib, tn)
    xflip = (dflip, tn)
    part = (dp, tflip)
    other = (dflip, tflip)
    up = (dp, a * NY + lax.rem(y + 1, NY))
    down = (dp, a * NY + lax.rem(y + NY - 1, NY))
    zpeer = [None] + [(xh * 16 + lax.rem(z + i, NZ) * 2 + c, tn) for i in range(1, NZ)]
    ring = (up, down)
    peers = [sib, xflip, part, other, up, down] + zpeer[1:]

    barrier = pltpu.get_barrier_semaphore()
    for peer in peers:
        pl.semaphore_signal(barrier, inc=1, device_id=peer, device_id_type=MESH)

    def local(i, src, dst):
        cp = pltpu.make_async_copy(src, dst, loc.at[i])
        cp.start()
        return cp

    lh = [local(t, hT.at[t], hin.at[t]) for t in range(STEPS)]
    lw = []
    for k in range(NC):
        cols = pl.ds((k % 2) * CW, CW)
        lw.append(local(4 + k, kv.at[k // 2, :, cols], wown.at[k]))
    lq = local(8, q, qin)
    lk = local(9, ck, kc.at[pl.ds(0, 16 * ROWS)])
    lv = local(10, cv, vc.at[pl.ds(0, 16 * ROWS)])

    count = [0]
    started = []

    def remote(src, dst, device):
        i = count[0]
        count[0] += 1
        cp = pltpu.make_async_remote_copy(
            src_ref=src, dst_ref=dst, send_sem=ssem.at[i], recv_sem=rsem.at[i],
            device_id=device, device_id_type=MESH,
        )
        cp.start()
        started.append(cp)
        return cp

    def transposed(into, wide, narrow, by_a, by_b):
        tpad[:, 0:DS] = wide[...] * by_a
        into[...] = tpad[...].T
        tpad[:, 0:R] = narrow[...] * by_b
        into[DS:GR, :] = tpad[:, 0:128].T[0:R, :]

    tpad[...] = jnp.zeros_like(tpad)
    transposed(gT, ga, gb, -rate_a, -rate_b)

    def pick(side, into):
        row = lax.broadcasted_iota(jnp.int32, (128, 16 * ROWS), 0)
        col = lax.broadcasted_iota(jnp.int32, (128, 16 * ROWS), 1)
        target = jnp.zeros((128, 16 * ROWS), jnp.int32)
        for i, j in enumerate(ORDER):
            first = (side * NY + lax.rem(y + j, NY)) * ROWS
            target = jnp.where(row >> 4 == i, first + (row & 15), target)
        sel = jnp.where((col == target) & ((row & 15) < ROWS), 1.0, 0.0).astype(BF)
        for t in range(STEPS):
            x = lax.dot_general(
                sel, hin[t], (((1,), (1,)), ((), ())), preferred_element_type=F32
            ).astype(BF)
            for i in range(8):
                into[i * TOK + 16 * t:i * TOK + 16 * t + 16, :] = x[16 * i:16 * i + 16, :]

    for cp in lh:
        cp.wait()
    pick(1 - a, hsend)
    pl.semaphore_wait(barrier, len(peers))

    krow = c * (DS // 2)

    def weight(k, lo, n, device):
        rows = pl.ds(pl.multiple_of(krow + lo, 16), n)
        return remote(wown.at[k, rows], wrem.at[k, rows], device)

    def forward(k):
        rows = pl.ds(pl.multiple_of(krow, 16), DS // 2)
        ref = wrem.at[k, rows]
        return remote(ref, ref, sib)

    def hidden(i):
        rows = pl.ds(i * TOK, TOK)
        return remote(hsend.at[rows], hrem.at[rows], part)

    mine = pl.multiple_of(c * GH, GH)
    theirs = pl.multiple_of((1 - c) * GH, GH)
    g1s[...] = gT[pl.ds(theirs, GH), :].astype(BF)
    g1 = remote(g1s, g1r, sib)
    lw[0].wait()
    w0a = weight(0, 0, 80, part)
    w0b = weight(0, 80, 80, other)
    hr = [hidden(i) for i in range(3)]
    lw[1].wait()
    w1 = weight(1, 0, 160, other)

    def product(k, lo, n):
        pk[k, lo:lo + n, :] = jnp.dot(
            hown[lo:lo + n, :], wown[k], preferred_element_type=F32
        ) + jnp.dot(hrem[lo:lo + n, :], wrem[k], preferred_element_type=F32)

    sent = {}

    def stage(k, s):
        if s == 0:
            for way in range(2):
                cut = slice(way * HALF, way * HALF + HALF)
                sb0[k, way] = pk[k, 0:TOK, cut].astype(BF)
                sent[k, 0, way] = remote(sb0.at[k, way], rb0.at[k, way], ring[way])
            return
        for way in range(2):
            lo = (2 * s - 1 + way) * TOK
            sent[k, s - 1, way].wait_recv()
            if s == 1:
                cut = slice(way * HALF, way * HALF + HALF)
                rest = slice((1 - way) * HALF, (1 - way) * HALF + HALF)
                sb[k, 0, way, :, cut] = (
                    pk[k, lo:lo + TOK, cut] + rb0[k, way].astype(F32)
                ).astype(BF)
                sb[k, 0, way, :, rest] = pk[k, lo:lo + TOK, rest].astype(BF)
            else:
                sb[k, s - 1, way] = (
                    pk[k, lo:lo + TOK, :] + rb[k, s - 2, way].astype(F32)
                ).astype(BF)
            sent[k, s, way] = remote(sb.at[k, s - 1, way], rb.at[k, s - 1, way], ring[way])

    def last(k, u, allb):
        for way in range(2):
            sent[k, 3, way].wait_recv()
        adapter = lax.dot_general(
            u[k // 2], allb[k % 2], (((1,), (1,)), ((), ())), preferred_element_type=F32
        )
        return (
            pk[k, 7 * TOK:, :] + rb[k, 2, 0].astype(F32) + rb[k, 2, 1].astype(F32) + adapter
        )

    def prepare_masks():
        i = lax.broadcasted_iota(jnp.int32, (256, 256), 0)
        j = lax.broadcasted_iota(jnp.int32, (256, 256), 1)
        length = jnp.zeros((256, 256), jnp.int32)
        for r in range(ROWS):
            length = jnp.where(j >> 4 == r, lens[r], length)
        ok = ((i & 15) == (j >> 4)) & ((j & 15) < length)
        biasc[...] = jnp.where(ok, 0.0, NEG)
        i = lax.broadcasted_iota(jnp.int32, (256, TOK), 0)
        j = lax.broadcasted_iota(jnp.int32, (256, TOK), 1)
        ok = ((i & 15) == (j & 15)) & (((i >> 4) & 3) >= (j >> 4))
        biasn[...] = jnp.where(ok, 0.0, NEG)

    def prepare_rotation():
        row = lax.broadcasted_iota(jnp.int32, (16, HD), 0)
        place = jnp.zeros((16, HD), jnp.int32)
        for r in range(ROWS):
            place = jnp.where(row == r, pos[r], place)
        lane = lax.broadcasted_iota(jnp.int32, (16, HD), 1)
        i = lane & 63
        coarse = jnp.zeros((16, HD), F32)
        fine = jnp.zeros((16, HD), F32)
        for n in range(8):
            coarse = jnp.where(i >> 3 == n, 1000000.0 ** (-16.0 * n / HD), coarse)
            fine = jnp.where((i & 7) == n, 1000000.0 ** (-2.0 * n / HD), fine)
        freq = coarse * fine
        sign = jnp.where(lane < 64, -1.0, 1.0)
        for t in range(STEPS):
            angle = (place + t).astype(F32) * freq
            cost[16 * t:16 * t + 16, :] = jnp.cos(angle)
            sint[16 * t:16 * t + 16, :] = jnp.sin(angle) * sign

    def prepare_queries():
        lq.wait()
        qs[...] = jnp.zeros_like(qs)
        for r in range(ROWS):
            row = qin[r].astype(F32)
            for n in range(QH):
                qs[n, pl.ds(r, STEPS, stride=16), :] = row[:, n * HD:n * HD + HD]
        for h in range(KVH):
            for g in range(4):
                qh[h, g * TOK:g * TOK + TOK, :] = qs[4 * h + g].astype(BF)

    def cached(h):
        cols = slice(h * HD, h * HD + HD)
        s = lax.dot_general(
            qh[h], kc[:, cols], (((1,), (1,)), ((), ())), preferred_element_type=F32
        ) * SCALE + biasc[...]
        top = jnp.max(s, axis=-1, keepdims=True)
        e = jnp.exp(s - top)
        mc[h] = top
        lc[h] = jnp.sum(e, axis=-1, keepdims=True)
        oc[h] = jnp.dot(e.astype(BF), vc[:, cols], preferred_element_type=F32)

    def new_keys(k, x):
        for n in range(4):
            h = 4 * k + n
            v = x[:, n * HD:n * HD + HD]
            v = v * lax.rsqrt(jnp.mean(v * v, axis=-1, keepdims=True) + 1e-06) * gain[...]
            turned = jnp.concatenate([v[:, 64:], v[:, :64]], axis=-1)
            key = (v * cost[...] + turned * sint[...]).astype(BF)
            s = lax.dot_general(
                qh[h], key, (((1,), (1,)), ((), ())), preferred_element_type=F32
            ) * SCALE + biasn[...]
            top = jnp.maximum(mc[h], jnp.max(s, axis=-1, keepdims=True))
            e = jnp.exp(s - top)
            back = jnp.exp(mc[h] - top)
            inv = 1.0 / (back * lc[h] + jnp.sum(e, axis=-1, keepdims=True))
            pn[h] = (e * inv).astype(BF)
            oc[h] = oc[h] * (back * inv)

    def new_values(k, x):
        for n in range(4):
            h = 4 * (k - 2) + n
            o = oc[h] + jnp.dot(
                pn[h], x[:, n * HD:n * HD + HD].astype(BF), preferred_element_type=F32
            )
            for g in range(4):
                of[4 * h + g] = o[g * TOK:g * TOK + TOK, :]
        for r in range(ROWS):
            for n in range(16 * (k - 2), 16 * (k - 1)):
                out[r, :, n * HD:n * HD + HD] = of[n, pl.ds(r, STEPS, stride=16), :].astype(BF)

    usent = {}

    def ustage(s):
        if s == 0:
            sbu[0, 0] = pu[0:TOK, :].astype(BF)
            usent[0, 0] = remote(sbu.at[0, 0], rbu.at[0, 0], up)
            return
        for way in range(2):
            lo = (2 * s - 1 + way) * TOK
            total = pu[lo:lo + TOK, :]
            if s > 1 or way == 0:
                usent[s - 1, way].wait_recv()
                total = total + rbu[s - 1, way].astype(F32)
            sbu[s, way] = total.astype(BF)
            usent[s, way] = remote(sbu.at[s, way], rbu.at[s, way], ring[way])

    bsent = {}

    def bstage(s):
        if s > 0:
            bsent[s - 1, 0].wait_recv()
            if s < 3:
                bsent[s - 1, 1].wait_recv()
        for way in range(2 if s < 3 else 1):
            from_y = lax.rem(y + NY - s, NY) if way == 0 else lax.rem(y + s, NY)
            ref = nball.at[c, from_y]
            bsent[s, way] = remote(ref, ref, ring[way])

    prepare_masks()
    pick(a, hown)
    g1.wait_recv()
    h2[...] = gT[pl.ds(mine, GH), :] + g1r[...].astype(F32)
    g3 = []
    for i in range(1, NZ):
        rows = pl.ds(pl.multiple_of(lax.rem(z + i, NZ) * GZ, GZ), GZ)
        g3.append(remote(h2.at[rows, :], g3r.at[i], zpeer[i]))
    transposed(fT, fa, fb, 0.5, 0.5)
    prepare_queries()

    w0a.wait_recv()
    w0b.wait_recv()
    f0 = forward(0)
    hr += [hidden(i) for i in range(3, 8)]
    lw[2].wait()
    w2 = weight(2, 0, 160, other)
    hr[0].wait_recv()
    f0.wait_recv()
    product(0, 0, TOK)
    stage(0, 0)
    kc[16 * ROWS:, :] = jnp.zeros((16, 1024), BF)
    vc[16 * ROWS:, :] = jnp.zeros((16, 1024), BF)
    lk.wait()
    lv.wait()
    w1.wait_recv()
    f1 = forward(1)
    lw[3].wait()
    w3 = [weight(3, 0, 80, part), weight(3, 80, 80, other)]
    for i in (1, 2):
        hr[i].wait_recv()
    product(0, TOK, 2 * TOK)
    f1.wait_recv()
    product(1, 0, TOK)
    stage(1, 0)
    stage(0, 1)

    piece = pl.ds(pl.multiple_of(c * GH + z * GZ, GZ), GZ)
    total = h2[pl.ds(pl.multiple_of(z * GZ, GZ), GZ), :] + fT[piece, :]
    for i in range(1, NZ):
        g3[i - 1].wait_recv()
        total = total + g3r[i]
    g2s[...] = total
    g2 = [remote(g2s, g2r.at[i], device) for i, device in enumerate((xflip, part, other))]

    product(1, TOK, 2 * TOK)
    stage(1, 1)
    cached(0)
    w2.wait_recv()
    f2 = forward(2)
    for i in (3, 4):
        hr[i].wait_recv()
    product(0, 3 * TOK, 2 * TOK)
    f2.wait_recv()
    product(2, 0, TOK)
    stage(2, 0)
    stage(0, 2)

    for cp in g2:
        cp.wait_recv()
    tot[c, z, a] = total + g2r[0]
    tot[c, z, 1 - a] = g2r[1] + g2r[2]
    g4 = [remote(tot.at[c, z], tot.at[c, z], zpeer[i]) for i in range(1, NZ)]

    for cp in w3:
        cp.wait_recv()
    f3 = forward(3)
    for i in (5, 6, 7):
        hr[i].wait_recv()
    f3.wait_recv()
    product(3, 0, TOK)
    stage(3, 0)
    product(1, 3 * TOK, 5 * TOK)
    stage(1, 2)
    product(2, TOK, 7 * TOK)
    stage(2, 1)
    product(0, 5 * TOK, 3 * TOK)
    stage(0, 3)
    product(3, TOK, 7 * TOK)
    cached(1)
    stage(3, 1)

    for cp in g4:
        cp.wait_recv()
    half = tot.at[c]
    g5 = remote(half, half, sib)
    cached(2)
    g5.wait_recv()
    def new_factors(side):
        return jnp.concatenate(
            [tot[core, i, side] for core in range(2) for i in range(NZ)], axis=0
        )

    full[0] = new_factors(a)
    full[1] = new_factors(1 - a)
    for i, side in ((0, a), (1, 1 - a)):
        nball[c, y, side] = full[i, pl.ds(pl.multiple_of(DS + c * 32, 32), 32), :].astype(BF)
    bstage(0)
    pu[...] = jnp.dot(
        hown[...], full[0, 0:DS, :].astype(BF), preferred_element_type=F32
    ) + jnp.dot(hrem[...], full[1, 0:DS, :].astype(BF), preferred_element_type=F32)
    ustage(0)
    stage(1, 3)
    cached(3)
    stage(2, 2)
    bstage(1)
    ustage(1)
    cached(4)
    stage(3, 2)
    cached(5)
    bstage(2)
    ustage(2)
    stage(2, 3)
    cached(6)
    bstage(3)
    ustage(3)
    stage(3, 3)
    cached(7)
    prepare_rotation()
    back = full[0].T
    na[...] = back[:, 0:DS]
    nb[...] = back[:, DS:GR]

    bsent[3, 0].wait_recv()
    bsent[2, 1].wait_recv()
    mineb = nball.at[c]
    shared = remote(mineb, mineb, sib)
    for way in range(2):
        usent[3, way].wait_recv()
    u = (pu[7 * TOK:, :] + rbu[3, 0].astype(F32) + rbu[3, 1].astype(F32)) * 0.25
    lane = lax.broadcasted_iota(jnp.int32, u.shape, 1)
    us = [jnp.where(lane >> 6 == p, u, 0.0).astype(BF) for p in range(2)]
    shared.wait_recv()
    allb = [
        jnp.concatenate([nball[core, i, side] for i in range(NY) for core in range(2)], axis=0)
        for side in range(2)
    ]
    new_keys(0, last(0, us, allb))
    new_keys(1, last(1, us, allb))
    new_values(2, last(2, us, allb))
    new_values(3, last(3, us, allb))
    for cp in started:
        cp.wait_send()


N_REMOTE = 6 + 4 + 8 + 32 + 7 + 1 + 7 + 3 + 7 + 1 + 7 + 1


def transfers(rate_a, rate_b, *operands):
    def body(*refs):
        transfer_kernel(rate_a, rate_b, *refs)

    vmem = pl.BlockSpec(memory_space=pltpu.VMEM)
    hbm = pl.BlockSpec(memory_space=pltpu.HBM)
    smem = pl.BlockSpec(memory_space=pltpu.SMEM)
    return pl.pallas_call(
        body,
        out_shape=(
            jax.ShapeDtypeStruct((ROWS, STEPS, QH * HD), BF),
            jax.ShapeDtypeStruct((2 * R, DS), F32),
            jax.ShapeDtypeStruct((2 * R, R), F32),
        ),
        in_specs=[hbm, hbm, vmem, vmem, vmem, vmem, vmem, hbm, hbm, hbm, smem, smem],
        out_specs=(vmem, vmem, vmem),
        scratch_shapes=[
            pltpu.VMEM((STEPS, DS, 16 * ROWS), BF),
            pltpu.VMEM((8 * TOK, DS), BF),
            pltpu.VMEM((8 * TOK, DS), BF),
            pltpu.VMEM((8 * TOK, DS), BF),
            pltpu.VMEM((NC, DS, CW), BF),
            pltpu.VMEM((NC, DS, CW), BF),
            pltpu.VMEM((NC, 8 * TOK, CW), F32),
            pltpu.VMEM((NC, 2, TOK, HALF), BF),
            pltpu.VMEM((NC, 2, TOK, HALF), BF),
            pltpu.VMEM((NC, 3, 2, TOK, CW), BF),
            pltpu.VMEM((NC, 3, 2, TOK, CW), BF),
            pltpu.VMEM((8 * TOK, 128), F32),
            pltpu.VMEM((4, 2, TOK, 128), BF),
            pltpu.VMEM((4, 2, TOK, 128), BF),
            pltpu.VMEM((128, GR), F32),
            pltpu.VMEM((GR, 128), F32),
            pltpu.VMEM((GR, 128), F32),
            pltpu.VMEM((GH, 128), BF),
            pltpu.VMEM((GH, 128), BF),
            pltpu.VMEM((GZ, 128), F32),
            pltpu.VMEM((3, GZ, 128), F32),
            pltpu.VMEM((GH, 128), F32),
            pltpu.VMEM((NZ, GZ, 128), F32),
            pltpu.VMEM((2, NZ, 2, GZ, 128), F32),
            pltpu.VMEM((2, GR, 128), F32),
            pltpu.VMEM((2, NY, 2, 32, 128), BF),
            pltpu.VMEM((ROWS, STEPS, QH * HD), BF),
            pltpu.VMEM((QH, TOK, HD), F32),
            pltpu.VMEM((KVH, 256, HD), BF),
            pltpu.VMEM((256, 1024), BF),
            pltpu.VMEM((256, 1024), BF),
            pltpu.VMEM((256, 256), F32),
            pltpu.VMEM((256, TOK), F32),
            pltpu.VMEM((TOK, HD), F32),
            pltpu.VMEM((TOK, HD), F32),
            pltpu.VMEM((KVH, 256, 1), F32),
            pltpu.VMEM((KVH, 256, 1), F32),
            pltpu.VMEM((KVH, 256, HD), F32),
            pltpu.VMEM((KVH, 256, TOK), BF),
            pltpu.VMEM((QH, TOK, HD), F32),
            pltpu.SemaphoreType.DMA((11,)),
            pltpu.SemaphoreType.DMA((N_REMOTE,)),
            pltpu.SemaphoreType.DMA((N_REMOTE,)),
        ],
        compiler_params=pltpu.CompilerParams(
            collective_id=0, has_side_effects=True, vmem_limit_bytes=56 * 1024 * 1024
        ),
    )(*operands)


def per_device(
    hidden_in, kv_weight, factor_a, factor_b, grad_a, grad_b, key_gain,
    queries, cache_keys, cache_values, cache_lengths, positions,
):
    groups_dp = lax.axis_size("dp")
    rate_a = 2.0 / math.sqrt(groups_dp * D)
    rate_b = 2.0 / math.sqrt(groups_dp * R)
    attended, na, nb = transfers(
        rate_a, rate_b, hidden_in.transpose(1, 2, 0), kv_weight,
        grad_a.reshape(2 * R, DS), grad_b.reshape(2 * R, R),
        factor_a.reshape(2 * R, DS), factor_b.reshape(2 * R, R),
        key_gain.reshape(1, HD), queries,
        cache_keys.reshape(16 * ROWS, KVH * HD), cache_values.reshape(16 * ROWS, KVH * HD),
        cache_lengths, positions,
    )
    return (attended, na.reshape(2, R, DS), nb.reshape(2, R, R))


def solution(mesh):
    return jax.shard_map(
        per_device,
        mesh=mesh,
        in_specs=(
            P("dp", None, "tensor"),
            P(None, "tensor", None),
            P(None, None, "tensor"),
            P(None, None, "tensor"),
            P("dp", None, None, "tensor"),
            P("dp", None, None, "tensor"),
            P(),
            P(("dp", "tensor"), None, None),
            P(("dp", "tensor"), None, None),
            P(("dp", "tensor"), None, None),
            P(("dp", "tensor")),
            P(("dp", "tensor")),
        ),
        out_specs=(
            P(("dp", "tensor"), None, None),
            P(None, None, "tensor"),
            P(None, None, "tensor"),
        ),
        check_vma=False,
    )
```

```python
import math

import jax
import jax.numpy as jnp
from jax import lax
from jax.experimental import pallas as pl
from jax.experimental.pallas import tpu as pltpu
from jax.sharding import PartitionSpec as P

D = 5120
KVH = 8
HD = 128
QH = 32
R = 64
STEPS = 4
KV = 2048
MESH = pl.DeviceIdType.MESH

NY = 8
NZ = 8
TOK = 64
DS = 320
ORDER = (4, 3, 5, 2, 6, 1, 7, 0)
NC = 5
WIDTH = (512, 256, 512, 512, 512)
PIECES = ((0,), (1,), (2, 3), (4, 5), (6, 7))
GR = 384
GP = 512
GH = GP // 2
GZ = GH // NZ
ROWS = 15
SCALE = HD ** -0.5
NEG = -1e30
F32 = jnp.float32
BF = jnp.bfloat16


def transfer_kernel(
    rate_a, rate_b,
    hT, kv, ga, gb, fa, fb, gain, q, ck, cv, lens, pos,
    out, na, nb,
    hin, hsend, hown, hrem, wfirst, wown, wrem, wnarrow, wnarrowr,
    pk, pknarrow, sb0, rb0, sb, rb, sb0l, rb0l, sbl, rbl, first, xs, xr,
    pu, sbu, rbu,
    gav, gbv, fav, fbv, tpad, gT, fT, g1s, g1r, h2, g3r, g2s, g2r, tot, nball, hball, b3r, b2s, b2r,
    qin, qs, qh, kc, vc, biasc, biasn, cost, sint, mc, lc, oc, pn, of, outv, nav, nbv,
    loc, ssem, rsem,
):
    dp = lax.axis_index("dp")
    tn = lax.axis_index("tensor")
    xh, z, c = dp // 16, lax.rem(dp // 2, 8), lax.rem(dp, 2)
    a, y = tn // NY, lax.rem(tn, NY)
    dflip = lax.rem(dp + 16, 32)
    tflip = lax.rem(tn + 8, 16)
    sib = (dp + 1 - 2 * c, tn)
    xflip = (dflip, tn)
    part = (dp, tflip)
    other = (dflip, tflip)
    ypeer = [None] + [(dp, a * NY + lax.rem(y + i, NY)) for i in range(1, NY)]
    zpeer = [None] + [(xh * 16 + lax.rem(z + i, NZ) * 2 + c, tn) for i in range(1, NZ)]
    ring = (ypeer[1], ypeer[NY - 1])
    peers = [sib, xflip, part, other] + ypeer[1:] + zpeer[1:]

    barrier = pltpu.get_barrier_semaphore()
    for peer in peers:
        pl.semaphore_signal(barrier, inc=1, device_id=peer, device_id_type=MESH)

    nloc = [0]

    def local(src, dst):
        cp = pltpu.make_async_copy(src, dst, loc.at[nloc[0]])
        nloc[0] += 1
        cp.start()
        return cp

    lh = [local(hT.at[t], hin.at[t]) for t in range(STEPS)]
    lw = [local(kv.at[0, :, pl.ds(0, 256)], wfirst), local(kv.at[0, :, pl.ds(256, 256)], wnarrow)]
    lg = [local(ga, gav), local(gb, gbv)]
    lw += [
        local(kv.at[0, :, pl.ds(512, 512)], wown.at[0]),
        local(kv.at[1, :, pl.ds(0, 512)], wown.at[1]),
        local(kv.at[1, :, pl.ds(512, 512)], wown.at[2]),
    ]
    lq = local(q, qin)
    lk = local(ck, kc.at[pl.ds(0, 16 * ROWS)])
    lv = local(cv, vc.at[pl.ds(0, 16 * ROWS)])
    lf = [local(fa, fav), local(fb, fbv)]

    count = [0]
    started = []

    def remote(src, dst, device):
        i = count[0]
        count[0] += 1
        cp = pltpu.make_async_remote_copy(
            src_ref=src, dst_ref=dst, send_sem=ssem.at[i], recv_sem=rsem.at[i],
            device_id=device, device_id_type=MESH,
        )
        cp.start()
        started.append(cp)
        return cp

    def transposed(into, wide, narrow, by_a, by_b):
        tpad[:, 0:DS] = wide[...] * by_a
        into[0:GR, :] = tpad[...].T
        tpad[:, 0:R] = narrow[...] * by_b
        into[DS:GR, :] = tpad[:, 0:128].T[0:R, :]

    def pick(side, into):
        row = lax.broadcasted_iota(jnp.int32, (128, 16 * ROWS), 0)
        col = lax.broadcasted_iota(jnp.int32, (128, 16 * ROWS), 1)
        target = jnp.zeros((128, 16 * ROWS), jnp.int32)
        for i, j in enumerate(ORDER):
            first = (side * NY + lax.rem(y + j, NY)) * ROWS
            target = jnp.where(row >> 4 == i, first + (row & 15), target)
        sel = jnp.where((col == target) & ((row & 15) < ROWS), 1.0, 0.0).astype(BF)
        for t in range(STEPS):
            x = lax.dot_general(
                sel, hin[t], (((1,), (1,)), ((), ())), preferred_element_type=F32
            ).astype(BF)
            for i in range(8):
                into[i * TOK + 16 * t:i * TOK + 16 * t + 16, :] = x[16 * i:16 * i + 16, :]

    wo = (None, wnarrow, wown.at[0], wown.at[1], wown.at[2])
    wr = (None, wnarrowr, wrem.at[0], wrem.at[1], wrem.at[2])
    krow = c * (DS // 2)

    def weight(k, lo, n, device):
        rows = pl.ds(pl.multiple_of(krow + lo, 16), n)
        return remote(wo[k].at[rows], wr[k].at[rows], device)

    def forward(k):
        ref = wr[k].at[pl.ds(pl.multiple_of(krow, 16), DS // 2)]
        return remote(ref, ref, sib)

    def hidden(i):
        rows = pl.ds(i * TOK, TOK)
        return remote(hsend.at[rows], hrem.at[rows], part)

    pks = [pk.at[0], pknarrow, pk.at[1], pk.at[2], pk.at[3]]

    def product(k, lo, n):
        rows = slice(lo, lo + n)
        if k == 0:
            pk[0, rows, 0:256] = jnp.dot(hown[rows, :], wfirst[...], preferred_element_type=F32)
            pk[0, rows, 256:512] = jnp.dot(hsend[rows, :], wfirst[...], preferred_element_type=F32)
            return
        pks[k][rows, :] = jnp.dot(
            hown[rows, :], wo[k][...], preferred_element_type=F32
        ) + jnp.dot(hrem[rows, :], wr[k][...], preferred_element_type=F32)

    def slot(k, s, way):
        n = max(k - 1, 0)
        if s == 0:
            return (sb0l.at[way], rb0l.at[way]) if k == 1 else (sb0.at[n, way], rb0.at[n, way])
        if k == 1:
            return sbl.at[s - 1, way], rbl.at[s - 1, way]
        return sb.at[n, s - 1, way], rb.at[n, s - 1, way]

    sent = {}

    def stage(k, s):
        half = WIDTH[k] // 2
        for way in range(2):
            src, dst = slot(k, s, way)
            cut = slice(way * half, way * half + half)
            rest = slice((1 - way) * half, (1 - way) * half + half)
            if s == 0:
                src[...] = pks[k][0:TOK, cut].astype(BF)
            else:
                rows = slice((2 * s - 1 + way) * TOK, (2 * s + way) * TOK)
                sent[k, s - 1, way].wait_recv()
                got = slot(k, s - 1, way)[1]
                if s == 1:
                    src[:, cut] = (pks[k][rows, cut] + got[...].astype(F32)).astype(BF)
                    src[:, rest] = pks[k][rows, rest].astype(BF)
                else:
                    src[...] = (pks[k][rows, :] + got[...].astype(F32)).astype(BF)
            sent[k, s, way] = remote(src, dst, ring[way])

    def last(k):
        total = pks[k][7 * TOK:8 * TOK, :]
        for way in range(2):
            sent[k, 3, way].wait_recv()
            total = total + slot(k, 3, way)[1][...].astype(F32)
        return total

    def adapter(j):
        return lax.dot_general(
            us[j // 4], allb[(j % 4) // 2][(j % 2) * 256:(j % 2) * 256 + 256],
            (((1,), (1,)), ((), ())), preferred_element_type=F32,
        )

    def prepare_masks():
        j = lax.broadcasted_iota(jnp.int32, (256, 256), 0)
        i = lax.broadcasted_iota(jnp.int32, (256, 256), 1)
        length = jnp.zeros((256, 256), jnp.int32)
        for r in range(ROWS):
            length = jnp.where(j >> 4 == r, lens[r], length)
        ok = ((i & 15) == (j >> 4)) & ((j & 15) < length)
        biasc[...] = jnp.where(ok, 0.0, NEG)
        j = lax.broadcasted_iota(jnp.int32, (TOK, 256), 0)
        i = lax.broadcasted_iota(jnp.int32, (TOK, 256), 1)
        ok = ((i & 15) == (j & 15)) & (((i >> 4) & 3) >= (j >> 4))
        biasn[...] = jnp.where(ok, 0.0, NEG)

    def prepare_rotation():
        row = lax.broadcasted_iota(jnp.int32, (16, HD), 0)
        place = jnp.zeros((16, HD), jnp.int32)
        for r in range(ROWS):
            place = jnp.where(row == r, pos[r], place)
        lane = lax.broadcasted_iota(jnp.int32, (16, HD), 1)
        i = lane & 63
        coarse = jnp.zeros((16, HD), F32)
        fine = jnp.zeros((16, HD), F32)
        for n in range(8):
            coarse = jnp.where(i >> 3 == n, 1000000.0 ** (-16.0 * n / HD), coarse)
            fine = jnp.where((i & 7) == n, 1000000.0 ** (-2.0 * n / HD), fine)
        freq = coarse * fine
        sign = jnp.where(lane < 64, -1.0, 1.0)
        for t in range(STEPS):
            angle = (place + t).astype(F32) * freq
            cost[16 * t:16 * t + 16, :] = jnp.cos(angle)
            sint[16 * t:16 * t + 16, :] = jnp.sin(angle) * sign

    def prepare_queries():
        lq.wait()
        qs[...] = jnp.zeros_like(qs)
        for r in range(ROWS):
            row = qin[r].astype(F32)
            for n in range(QH):
                qs[n, pl.ds(r, STEPS, stride=16), :] = row[:, n * HD:n * HD + HD]
        for h in range(KVH):
            for g in range(4):
                qh[h, g * TOK:g * TOK + TOK, :] = qs[4 * h + g].astype(BF)

    def cached(h):
        cols = slice(h * HD, h * HD + HD)
        s = lax.dot_general(
            kc[:, cols], qh[h], (((1,), (1,)), ((), ())), preferred_element_type=F32
        ) * SCALE + biasc[...]
        top = jnp.max(s, axis=0, keepdims=True)
        e = jnp.exp(s - top)
        mc[h] = top
        lc[h] = jnp.sum(e, axis=0, keepdims=True)
        oc[h] = lax.dot_general(
            vc[:, cols], e.astype(BF), (((0,), (0,)), ((), ())), preferred_element_type=F32
        )

    def new_keys(j, x):
        for n in range(2):
            h = 2 * j + n
            v = x[:, n * HD:n * HD + HD]
            v = v * lax.rsqrt(jnp.mean(v * v, axis=-1, keepdims=True) + 1e-06) * gain[...]
            turned = jnp.concatenate([v[:, 64:], v[:, :64]], axis=-1)
            key = (v * cost[...] + turned * sint[...]).astype(BF)
            s = lax.dot_general(
                key, qh[h], (((1,), (1,)), ((), ())), preferred_element_type=F32
            ) * SCALE + biasn[...]
            top = jnp.maximum(mc[h], jnp.max(s, axis=0, keepdims=True))
            e = jnp.exp(s - top)
            back = jnp.exp(mc[h] - top)
            inv = 1.0 / (back * lc[h] + jnp.sum(e, axis=0, keepdims=True))
            pn[h] = (e * inv).astype(BF)
            oc[h] = oc[h] * (back * inv)

    lo_ = []

    def new_values(j, x):
        for n in range(2):
            h = 2 * (j - 4) + n
            o = oc[h] + lax.dot_general(
                x[:, n * HD:n * HD + HD].astype(BF), pn[h], (((0,), (0,)), ((), ())),
                preferred_element_type=F32,
            )
            o = o.T
            for g in range(4):
                of[4 * h + g] = o[g * TOK:g * TOK + TOK, :]
        for r in range(ROWS):
            for n in range(8 * (j - 4), 8 * (j - 3)):
                outv[r, :, n * HD:n * HD + HD] = of[n, pl.ds(r, STEPS, stride=16), :].astype(BF)
        cols = pl.ds((j - 4) * 1024, 1024)
        lo_.append(local(outv.at[:, :, cols], out.at[:, :, cols]))

    tpad[...] = jnp.zeros_like(tpad)
    gT[GR:, :] = jnp.zeros((GP - GR, 128), F32)
    mine = pl.multiple_of(c * GH, GH)
    theirs = pl.multiple_of((1 - c) * GH, GH)
    for cp in lg:
        cp.wait()
    transposed(gT, gav, gbv, -rate_a, -rate_b)
    g1s[0:GH, :] = gT[pl.ds(theirs, GH), :].astype(BF)
    bmine = pl.ds(pl.multiple_of(DS + c * 32, 32), 32)
    btheirs = pl.ds(pl.multiple_of(DS + (1 - c) * 32, 32), 32)
    g1s[GH:, :] = gT[btheirs, :].astype(BF)
    for cp in lh:
        cp.wait()
    pick(a, hown)
    pick(1 - a, hsend)
    lw[0].wait()
    product(0, 0, TOK)
    pl.semaphore_wait(barrier, len(peers))

    g1 = remote(g1s, g1r, sib)
    stage(0, 0)
    lw[1].wait()
    w1 = [weight(1, 0, 80, part), weight(1, 80, 80, other)]
    hr = [hidden(0)]
    lw[2].wait()
    w2 = weight(2, 0, 160, other)
    hr += [hidden(i) for i in range(1, 5)]

    g1.wait_recv()
    h2[...] = (gT[pl.ds(mine, GH), :] + g1r[0:GH, :].astype(F32)).astype(BF)
    g3 = []
    for i in range(1, NZ):
        rows = pl.ds(pl.multiple_of(lax.rem(z + i, NZ) * GZ, GZ), GZ)
        g3.append(remote(h2.at[rows, :], g3r.at[i], zpeer[i]))
    product(0, TOK, 7 * TOK)
    for cp in lf:
        cp.wait()
    fT[GR:, :] = jnp.zeros((GP - GR, 128), F32)
    transposed(fT, fav, fbv, 0.5, 0.5)
    hball[y] = (
        gT[bmine, :] + g1r[GH:, :].astype(F32) + fT[bmine, :] * 0.125
    ).astype(BF)
    b0 = [remote(hball.at[y], hball.at[y], ypeer[i]) for i in range(1, NY)]
    stage(0, 1)

    for cp in w1:
        cp.wait_recv()
    f1 = forward(1)
    lw[3].wait()
    w3 = weight(3, 0, 160, other)
    lw[4].wait()
    w4 = [weight(4, 0, 80, part)]
    hr += [hidden(i) for i in range(5, 8)]
    w4.append(weight(4, 80, 80, other))
    prepare_masks()
    hr[0].wait_recv()
    f1.wait_recv()
    product(1, 0, TOK)
    stage(1, 0)
    for i in (1, 2):
        hr[i].wait_recv()
    product(1, TOK, 2 * TOK)
    w2.wait_recv()
    f2 = forward(2)
    stage(0, 2)

    piece = pl.ds(pl.multiple_of(c * GH + z * GZ, GZ), GZ)
    total = h2[pl.ds(pl.multiple_of(z * GZ, GZ), GZ), :].astype(F32) + fT[piece, :]
    for i in range(1, NZ):
        g3[i - 1].wait_recv()
        total = total + g3r[i].astype(F32)
    g2s[...] = total
    g2 = [remote(g2s, g2r.at[i], device) for i, device in enumerate((xflip, part, other))]
    for cp in b0:
        cp.wait_recv()
    b3 = [
        remote(hball.at[lax.rem(z + i, NZ)], b3r.at[i], zpeer[i]) for i in range(1, NZ)
    ]

    f2.wait_recv()
    product(2, 0, TOK)
    stage(2, 0)
    stage(1, 1)
    prepare_queries()
    kc[16 * ROWS:, :] = jnp.zeros((16, 1024), BF)
    vc[16 * ROWS:, :] = jnp.zeros((16, 1024), BF)
    for i in (3, 4):
        hr[i].wait_recv()
    product(2, TOK, 4 * TOK)
    w3.wait_recv()
    f3 = forward(3)
    stage(0, 3)
    product(1, 3 * TOK, 2 * TOK)
    f3.wait_recv()
    product(3, 0, TOK)
    stage(3, 0)

    for cp in g2:
        cp.wait_recv()
    tot[c, z, a] = (g2s[...] + g2r[0]).astype(BF)
    tot[c, z, 1 - a] = (g2r[1] + g2r[2]).astype(BF)
    g4 = [remote(tot.at[c, z], tot.at[c, z], zpeer[i]) for i in range(1, NZ)]

    stage(2, 1)
    stage(1, 2)
    for cp in w4:
        cp.wait_recv()
    f4 = forward(4)
    lk.wait()
    lv.wait()
    total = last(0)
    xs[...] = total[:, 256:512].astype(BF)
    x0 = remote(xs, xr, part)
    first[...] = total[:, 0:256]
    total = hball[z].astype(F32)
    for i in range(1, NZ):
        b3[i - 1].wait_recv()
        total = total + b3r[i].astype(F32)
    b2s[...] = total
    b2 = [remote(b2s, b2r.at[i], device) for i, device in enumerate((xflip, part, other))]
    product(3, TOK, 4 * TOK)
    f4.wait_recv()
    product(4, 0, TOK)
    stage(4, 0)
    stage(3, 1)
    for cp in g4:
        cp.wait_recv()
    g5 = remote(tot.at[c], tot.at[c], sib)
    for i in (5, 6, 7):
        hr[i].wait_recv()
    product(2, 5 * TOK, 3 * TOK)
    stage(2, 2)
    g5.wait_recv()

    def new_a(side):
        return jnp.concatenate([tot[e // NZ, e % NZ, side] for e in range(10)], axis=0)

    pu[...] = jnp.dot(hown[...], new_a(a), preferred_element_type=F32) + jnp.dot(
        hrem[...], new_a(1 - a), preferred_element_type=F32
    )
    u1 = []
    for i in range(7):
        sbu[i] = pu[i * TOK:(i + 1) * TOK, :].astype(BF)
        u1.append(remote(sbu.at[i], rbu.at[i], ypeer[ORDER[i]]))
    for cp in b2:
        cp.wait_recv()
    nball[c, z, a] = (b2s[...] + b2r[0]).astype(BF)
    nball[c, z, 1 - a] = (b2r[1] + b2r[2]).astype(BF)
    b4 = [remote(nball.at[c, z], nball.at[c, z], zpeer[i]) for i in range(1, NZ)]
    product(1, 5 * TOK, 3 * TOK)
    stage(1, 3)
    product(4, TOK, 7 * TOK)
    stage(4, 1)
    product(3, 5 * TOK, 3 * TOK)
    stage(3, 2)
    cached(0)
    stage(2, 3)
    cached(1)

    stage(4, 2)
    stage(3, 3)
    for cp in b4:
        cp.wait_recv()
    b5 = remote(nball.at[c], nball.at[c], sib)
    cached(2)
    stage(4, 3)
    cached(3)
    for h in range(4, KVH):
        cached(h)
    prepare_rotation()
    back = jnp.concatenate([tot[e // NZ, e % NZ, a].astype(F32) for e in range(12)], axis=0).T
    nav[...] = back[:, 0:DS]
    lo_ += [local(nav, na)]

    u = pu[7 * TOK:, :]
    for i in range(7):
        u1[i].wait_recv()
        u = u + rbu[i].astype(F32)
    u = u * 0.25
    lane = lax.broadcasted_iota(jnp.int32, u.shape, 1)
    us = [jnp.where(lane >> 6 == p, u, 0.0).astype(BF) for p in range(2)]
    x0.wait_recv()
    b5.wait_recv()
    back = jnp.concatenate(
        [nball[0, y, a].astype(F32), nball[1, y, a].astype(F32), jnp.zeros((64, 128), F32)], axis=0
    ).T
    nbv[...] = back[:, 0:R]
    lo_ += [local(nbv, nb)]
    allb = [
        jnp.concatenate([nball[core, i, side] for i in range(NY) for core in range(2)], axis=0)
        for side in range(2)
    ]
    new_keys(0, first[...] + xr[...].astype(F32) + adapter(0))
    for k in range(1, NC):
        total = last(k)
        for n, j in enumerate(PIECES[k]):
            x = total[:, n * 256:n * 256 + 256] + adapter(j)
            if j < 4:
                new_keys(j, x)
            else:
                new_values(j, x)
    assert count[0] == N_REMOTE and nloc[0] == N_LOCAL
    for cp in lo_:
        cp.wait()
    for cp in started:
        cp.wait_send()


N_LOCAL = 22
N_REMOTE = 6 + 4 + 8 + 40 + 7 + 1 + 7 + 3 + 7 + 1 + 1 + 7 + 7 + 3 + 7 + 1


def transfers(rate_a, rate_b, *operands):
    def body(*refs):
        transfer_kernel(rate_a, rate_b, *refs)

    vmem = pl.BlockSpec(memory_space=pltpu.VMEM)
    hbm = pl.BlockSpec(memory_space=pltpu.HBM)
    smem = pl.BlockSpec(memory_space=pltpu.SMEM)
    return pl.pallas_call(
        body,
        out_shape=(
            jax.ShapeDtypeStruct((ROWS, STEPS, QH * HD), BF),
            jax.ShapeDtypeStruct((2 * R, DS), F32),
            jax.ShapeDtypeStruct((2 * R, R), F32),
        ),
        in_specs=[hbm] * 6 + [vmem, hbm, hbm, hbm, smem, smem],
        out_specs=(hbm, hbm, hbm),
        scratch_shapes=[
            pltpu.VMEM((STEPS, DS, 16 * ROWS), BF),
            pltpu.VMEM((8 * TOK, DS), BF),
            pltpu.VMEM((8 * TOK, DS), BF),
            pltpu.VMEM((8 * TOK, DS), BF),
            pltpu.VMEM((DS, 256), BF),
            pltpu.VMEM((3, DS, 512), BF),
            pltpu.VMEM((3, DS, 512), BF),
            pltpu.VMEM((DS, 256), BF),
            pltpu.VMEM((DS, 256), BF),
            pltpu.VMEM((4, 8 * TOK, 512), F32),
            pltpu.VMEM((8 * TOK, 256), F32),
            pltpu.VMEM((4, 2, TOK, 256), BF),
            pltpu.VMEM((4, 2, TOK, 256), BF),
            pltpu.VMEM((4, 3, 2, TOK, 512), BF),
            pltpu.VMEM((4, 3, 2, TOK, 512), BF),
            pltpu.VMEM((2, TOK, 128), BF),
            pltpu.VMEM((2, TOK, 128), BF),
            pltpu.VMEM((3, 2, TOK, 256), BF),
            pltpu.VMEM((3, 2, TOK, 256), BF),
            pltpu.VMEM((TOK, 256), F32),
            pltpu.VMEM((TOK, 256), BF),
            pltpu.VMEM((TOK, 256), BF),
            pltpu.VMEM((8 * TOK, 128), F32),
            pltpu.VMEM((7, TOK, 128), BF),
            pltpu.VMEM((7, TOK, 128), BF),
            pltpu.VMEM((2 * R, DS), F32),
            pltpu.VMEM((2 * R, R), F32),
            pltpu.VMEM((2 * R, DS), F32),
            pltpu.VMEM((2 * R, R), F32),
            pltpu.VMEM((128, GR), F32),
            pltpu.VMEM((GP, 128), F32),
            pltpu.VMEM((GP, 128), F32),
            pltpu.VMEM((GH + 32, 128), BF),
            pltpu.VMEM((GH + 32, 128), BF),
            pltpu.VMEM((GH, 128), BF),
            pltpu.VMEM((NZ, GZ, 128), BF),
            pltpu.VMEM((GZ, 128), F32),
            pltpu.VMEM((3, GZ, 128), F32),
            pltpu.VMEM((2, NZ, 2, GZ, 128), BF),
            pltpu.VMEM((2, NY, 2, 32, 128), BF),
            pltpu.VMEM((NY, 32, 128), BF),
            pltpu.VMEM((NZ, 32, 128), BF),
            pltpu.VMEM((32, 128), F32),
            pltpu.VMEM((3, 32, 128), F32),
            pltpu.VMEM((ROWS, STEPS, QH * HD), BF),
            pltpu.VMEM((QH, TOK, HD), F32),
            pltpu.VMEM((KVH, 256, HD), BF),
            pltpu.VMEM((256, 1024), BF),
            pltpu.VMEM((256, 1024), BF),
            pltpu.VMEM((256, 256), F32),
            pltpu.VMEM((TOK, 256), F32),
            pltpu.VMEM((TOK, HD), F32),
            pltpu.VMEM((TOK, HD), F32),
            pltpu.VMEM((KVH, 1, 256), F32),
            pltpu.VMEM((KVH, 1, 256), F32),
            pltpu.VMEM((KVH, HD, 256), F32),
            pltpu.VMEM((KVH, TOK, 256), BF),
            pltpu.VMEM((QH, TOK, HD), F32),
            pltpu.VMEM((ROWS, STEPS, QH * HD), BF),
            pltpu.VMEM((2 * R, DS), F32),
            pltpu.VMEM((2 * R, R), F32),
            pltpu.SemaphoreType.DMA((N_LOCAL,)),
            pltpu.SemaphoreType.DMA((N_REMOTE,)),
            pltpu.SemaphoreType.DMA((N_REMOTE,)),
        ],
        compiler_params=pltpu.CompilerParams(
            collective_id=0, has_side_effects=True, vmem_limit_bytes=56 * 1024 * 1024
        ),
    )(*operands)


def results_kernel(att, na, nb, att_out, na_out, nb_out, attv, nav, nbv, sem):
    parts = [(att.at[pl.ds(3 * i, 3)], attv.at[pl.ds(3 * i, 3)], att_out.at[pl.ds(3 * i, 3)])
             for i in range(5)]
    parts += [(na, nav, na_out), (nb, nbv, nb_out)]
    reads = [pltpu.make_async_copy(x, v, sem.at[0, i]) for i, (x, v, _) in enumerate(parts)]
    writes = [pltpu.make_async_copy(v, o, sem.at[1, i]) for i, (_, v, o) in enumerate(parts)]
    for cp in reads:
        cp.start()
    for read, write in zip(reads, writes):
        read.wait()
        write.start()
    for cp in writes:
        cp.wait()


def results(*operands):
    hbm = pl.BlockSpec(memory_space=pltpu.HBM)
    return pl.pallas_call(
        results_kernel,
        out_shape=tuple(jax.ShapeDtypeStruct(x.shape, x.dtype) for x in operands),
        in_specs=[hbm] * 3,
        out_specs=(hbm,) * 3,
        scratch_shapes=[pltpu.VMEM(x.shape, x.dtype) for x in operands]
        + [pltpu.SemaphoreType.DMA((2, 7))],
        compiler_params=pltpu.CompilerParams(vmem_limit_bytes=56 * 1024 * 1024),
    )(*operands)


def per_device(
    hidden_in, kv_weight, factor_a, factor_b, grad_a, grad_b, key_gain,
    queries, cache_keys, cache_values, cache_lengths, positions,
):
    groups_dp = lax.axis_size("dp")
    rate_a = 2.0 / math.sqrt(groups_dp * D)
    rate_b = 2.0 / math.sqrt(groups_dp * R)
    attended, na, nb = results(*transfers(
        rate_a, rate_b, hidden_in.transpose(1, 2, 0), kv_weight,
        grad_a.reshape(2 * R, DS), grad_b.reshape(2 * R, R),
        factor_a.reshape(2 * R, DS), factor_b.reshape(2 * R, R),
        key_gain.reshape(1, HD), queries,
        cache_keys.reshape(16 * ROWS, KVH * HD), cache_values.reshape(16 * ROWS, KVH * HD),
        cache_lengths, positions,
    ))
    return (attended, na.reshape(2, R, DS), nb.reshape(2, R, R))


def solution(mesh):
    return jax.shard_map(
        per_device,
        mesh=mesh,
        in_specs=(
            P("dp", None, "tensor"),
            P(None, "tensor", None),
            P(None, None, "tensor"),
            P(None, None, "tensor"),
            P("dp", None, None, "tensor"),
            P("dp", None, None, "tensor"),
            P(),
            P(("dp", "tensor"), None, None),
            P(("dp", "tensor"), None, None),
            P(("dp", "tensor"), None, None),
            P(("dp", "tensor")),
            P(("dp", "tensor")),
        ),
        out_specs=(
            P(("dp", "tensor"), None, None),
            P(None, None, "tensor"),
            P(None, None, "tensor"),
        ),
        check_vma=False,
    )
```

```python
import math

import jax
import jax.numpy as jnp
from jax import lax
from jax.experimental import pallas as pl
from jax.experimental.pallas import tpu as pltpu
from jax.sharding import PartitionSpec as P

D = 5120
KVH = 8
HD = 128
QH = 32
R = 64
STEPS = 4
KV = 2048
MESH = pl.DeviceIdType.MESH

NY = 8
NZ = 8
TOK = 64
DS = 320
ORDER = (4, 3, 5, 2, 6, 1, 7, 0)
NC = 5
WIDTH = (512, 256, 512, 512, 512)
PIECES = ((0,), (1,), (2, 3), (4, 5), (6, 7))
GR = 384
GP = 512
GH = GP // 2
GZ = GH // NZ
ROWS = 15
SCALE = HD ** -0.5
NEG = -1e30
F32 = jnp.float32
BF = jnp.bfloat16


def transfer_kernel(
    rate_a, rate_b,
    hT, kv, ga, gb, fa, fb, gain, q, ck, cv, lens, pos,
    out, na, nb,
    hin, hsend, hown, hrem, wfirst, wown, wrem, wnarrow, wnarrowr,
    pk, pknarrow, sb0, rb0, sb, rb, sb0l, rb0l, sbl, rbl, first, xs, xr,
    pu, sbu, rbu,
    gav, gbv, fav, fbv, tpad, gT, fT, g1s, g1r, h2, g3r, g2s, g2r, tot, nball, hball, b3r, b2s, b2r,
    qin, qs, qh, kc, vc, biasc, biasn, cost, sint, mc, lc, oc, pn, of, outv, nav, nbv,
    loc, ssem, rsem,
):
    dp = lax.axis_index("dp")
    tn = lax.axis_index("tensor")
    xh, z, c = dp // 16, lax.rem(dp // 2, 8), lax.rem(dp, 2)
    a, y = tn // NY, lax.rem(tn, NY)
    dflip = lax.rem(dp + 16, 32)
    tflip = lax.rem(tn + 8, 16)
    sib = (dp + 1 - 2 * c, tn)
    xflip = (dflip, tn)
    part = (dp, tflip)
    other = (dflip, tflip)
    ypeer = [None] + [(dp, a * NY + lax.rem(y + i, NY)) for i in range(1, NY)]
    zpeer = [None] + [(xh * 16 + lax.rem(z + i, NZ) * 2 + c, tn) for i in range(1, NZ)]
    ring = (ypeer[1], ypeer[NY - 1])
    peers = [sib, xflip, part, other] + ypeer[1:] + zpeer[1:]

    barrier = pltpu.get_barrier_semaphore()
    for peer in peers:
        pl.semaphore_signal(barrier, inc=1, device_id=peer, device_id_type=MESH)

    nloc = [0]

    def local(src, dst):
        cp = pltpu.make_async_copy(src, dst, loc.at[nloc[0]])
        nloc[0] += 1
        cp.start()
        return cp

    lh = [local(hT.at[t], hin.at[t]) for t in range(STEPS)]
    lw = [local(kv.at[0, :, pl.ds(0, 256)], wfirst), local(kv.at[0, :, pl.ds(256, 256)], wnarrow)]
    lg = [local(ga, gav), local(gb, gbv)]
    lw += [
        local(kv.at[0, :, pl.ds(512, 512)], wown.at[0]),
        local(kv.at[1, :, pl.ds(0, 512)], wown.at[1]),
        local(kv.at[1, :, pl.ds(512, 512)], wown.at[2]),
    ]
    lq = local(q, qin)
    lk = local(ck, kc.at[pl.ds(0, 16 * ROWS)])
    lv = local(cv, vc.at[pl.ds(0, 16 * ROWS)])
    lf = [local(fa, fav), local(fb, fbv)]

    count = [0]
    started = []

    def remote(src, dst, device):
        i = count[0]
        count[0] += 1
        cp = pltpu.make_async_remote_copy(
            src_ref=src, dst_ref=dst, send_sem=ssem.at[i], recv_sem=rsem.at[i],
            device_id=device, device_id_type=MESH,
        )
        cp.start()
        started.append(cp)
        return cp

    def transposed(into, wide, narrow, by_a, by_b):
        tpad[:, 0:DS] = wide[...] * by_a
        into[0:GR, :] = tpad[...].T
        tpad[:, 0:R] = narrow[...] * by_b
        into[DS:GR, :] = tpad[:, 0:128].T[0:R, :]

    def pick(side, into):
        row = lax.broadcasted_iota(jnp.int32, (128, 16 * ROWS), 0)
        col = lax.broadcasted_iota(jnp.int32, (128, 16 * ROWS), 1)
        target = jnp.zeros((128, 16 * ROWS), jnp.int32)
        for i, j in enumerate(ORDER):
            first = (side * NY + lax.rem(y + j, NY)) * ROWS
            target = jnp.where(row >> 4 == i, first + (row & 15), target)
        sel = jnp.where((col == target) & ((row & 15) < ROWS), 1.0, 0.0).astype(BF)
        for t in range(STEPS):
            x = lax.dot_general(
                sel, hin[t], (((1,), (1,)), ((), ())), preferred_element_type=F32
            ).astype(BF)
            for i in range(8):
                into[i * TOK + 16 * t:i * TOK + 16 * t + 16, :] = x[16 * i:16 * i + 16, :]

    wo = (None, wnarrow, wown.at[0], wown.at[1], wown.at[2])
    wr = (None, wnarrowr, wrem.at[0], wrem.at[1], wrem.at[2])
    krow = c * (DS // 2)

    def weight(k, lo, n, device):
        rows = pl.ds(pl.multiple_of(krow + lo, 16), n)
        return remote(wo[k].at[rows], wr[k].at[rows], device)

    def forward(k):
        ref = wr[k].at[pl.ds(pl.multiple_of(krow, 16), DS // 2)]
        return remote(ref, ref, sib)

    def hidden(i):
        rows = pl.ds(i * TOK, TOK)
        return remote(hsend.at[rows], hrem.at[rows], part)

    pks = [pk.at[0], pknarrow, pk.at[1], pk.at[2], pk.at[3]]

    def product(k, lo, n):
        rows = slice(lo, lo + n)
        if k == 0:
            pk[0, rows, 0:256] = jnp.dot(hown[rows, :], wfirst[...], preferred_element_type=F32)
            pk[0, rows, 256:512] = jnp.dot(hsend[rows, :], wfirst[...], preferred_element_type=F32)
            return
        pks[k][rows, :] = jnp.dot(
            hown[rows, :], wo[k][...], preferred_element_type=F32
        ) + jnp.dot(hrem[rows, :], wr[k][...], preferred_element_type=F32)

    def slot(k, s, way):
        n = max(k - 1, 0)
        if s == 0:
            return (sb0l.at[way], rb0l.at[way]) if k == 1 else (sb0.at[n, way], rb0.at[n, way])
        if k == 1:
            return sbl.at[s - 1, way], rbl.at[s - 1, way]
        return sb.at[n, s - 1, way], rb.at[n, s - 1, way]

    sent = {}

    def stage(k, s):
        half = WIDTH[k] // 2
        for way in range(2):
            src, dst = slot(k, s, way)
            cut = slice(way * half, way * half + half)
            rest = slice((1 - way) * half, (1 - way) * half + half)
            if s == 0:
                src[...] = pks[k][0:TOK, cut].astype(BF)
            else:
                rows = slice((2 * s - 1 + way) * TOK, (2 * s + way) * TOK)
                sent[k, s - 1, way].wait_recv()
                got = slot(k, s - 1, way)[1]
                if s == 1:
                    src[:, cut] = (pks[k][rows, cut] + got[...].astype(F32)).astype(BF)
                    src[:, rest] = pks[k][rows, rest].astype(BF)
                else:
                    src[...] = (pks[k][rows, :] + got[...].astype(F32)).astype(BF)
            sent[k, s, way] = remote(src, dst, ring[way])

    def last(k):
        total = pks[k][7 * TOK:8 * TOK, :]
        for way in range(2):
            sent[k, 3, way].wait_recv()
            total = total + slot(k, 3, way)[1][...].astype(F32)
        return total

    def adapter(j):
        return lax.dot_general(
            us[j // 4], allb[(j % 4) // 2][(j % 2) * 256:(j % 2) * 256 + 256],
            (((1,), (1,)), ((), ())), preferred_element_type=F32,
        )

    usent = {}

    def ustage(s):
        if s == 0:
            sbu[0, 0] = pu[0:TOK, :].astype(BF)
            usent[0, 0] = remote(sbu.at[0, 0], rbu.at[0, 0], ring[0])
            return
        for way in range(2):
            total = pu[(2 * s - 1 + way) * TOK:(2 * s + way) * TOK, :]
            if s > 1 or way == 0:
                usent[s - 1, way].wait_recv()
                total = total + rbu[s - 1, way].astype(F32)
            sbu[s, way] = total.astype(BF)
            usent[s, way] = remote(sbu.at[s, way], rbu.at[s, way], ring[way])

    def prepare_masks():
        j = lax.broadcasted_iota(jnp.int32, (256, 256), 0)
        i = lax.broadcasted_iota(jnp.int32, (256, 256), 1)
        length = jnp.zeros((256, 256), jnp.int32)
        for r in range(ROWS):
            length = jnp.where(j >> 4 == r, lens[r], length)
        ok = ((i & 15) == (j >> 4)) & ((j & 15) < length)
        biasc[...] = jnp.where(ok, 0.0, NEG)
        j = lax.broadcasted_iota(jnp.int32, (TOK, 256), 0)
        i = lax.broadcasted_iota(jnp.int32, (TOK, 256), 1)
        ok = ((i & 15) == (j & 15)) & (((i >> 4) & 3) >= (j >> 4))
        biasn[...] = jnp.where(ok, 0.0, NEG)

    def prepare_rotation():
        row = lax.broadcasted_iota(jnp.int32, (16, HD), 0)
        place = jnp.zeros((16, HD), jnp.int32)
        for r in range(ROWS):
            place = jnp.where(row == r, pos[r], place)
        lane = lax.broadcasted_iota(jnp.int32, (16, HD), 1)
        i = lane & 63
        coarse = jnp.zeros((16, HD), F32)
        fine = jnp.zeros((16, HD), F32)
        for n in range(8):
            coarse = jnp.where(i >> 3 == n, 1000000.0 ** (-16.0 * n / HD), coarse)
            fine = jnp.where((i & 7) == n, 1000000.0 ** (-2.0 * n / HD), fine)
        freq = coarse * fine
        sign = jnp.where(lane < 64, -1.0, 1.0)
        for t in range(STEPS):
            angle = (place + t).astype(F32) * freq
            cost[16 * t:16 * t + 16, :] = jnp.cos(angle)
            sint[16 * t:16 * t + 16, :] = jnp.sin(angle) * sign

    def prepare_queries():
        lq.wait()
        qs[...] = jnp.zeros_like(qs)
        for r in range(ROWS):
            row = qin[r].astype(F32)
            for n in range(QH):
                qs[n, pl.ds(r, STEPS, stride=16), :] = row[:, n * HD:n * HD + HD]
        for h in range(KVH):
            for g in range(4):
                qh[h, g * TOK:g * TOK + TOK, :] = qs[4 * h + g].astype(BF)

    def cached(h):
        cols = slice(h * HD, h * HD + HD)
        s = lax.dot_general(
            kc[:, cols], qh[h], (((1,), (1,)), ((), ())), preferred_element_type=F32
        ) * SCALE + biasc[...]
        top = jnp.max(s, axis=0, keepdims=True)
        e = jnp.exp(s - top)
        mc[h] = top
        lc[h] = jnp.sum(e, axis=0, keepdims=True)
        oc[h] = lax.dot_general(
            vc[:, cols], e.astype(BF), (((0,), (0,)), ((), ())), preferred_element_type=F32
        )

    def new_keys(j, x):
        for n in range(2):
            h = 2 * j + n
            v = x[:, n * HD:n * HD + HD]
            v = v * lax.rsqrt(jnp.mean(v * v, axis=-1, keepdims=True) + 1e-06) * gain[...]
            turned = jnp.concatenate([v[:, 64:], v[:, :64]], axis=-1)
            key = (v * cost[...] + turned * sint[...]).astype(BF)
            s = lax.dot_general(
                key, qh[h], (((1,), (1,)), ((), ())), preferred_element_type=F32
            ) * SCALE + biasn[...]
            top = jnp.maximum(mc[h], jnp.max(s, axis=0, keepdims=True))
            e = jnp.exp(s - top)
            back = jnp.exp(mc[h] - top)
            inv = 1.0 / (back * lc[h] + jnp.sum(e, axis=0, keepdims=True))
            pn[h] = (e * inv).astype(BF)
            oc[h] = oc[h] * (back * inv)

    lo_ = []

    def new_values(j, x):
        for n in range(2):
            h = 2 * (j - 4) + n
            o = oc[h] + lax.dot_general(
                x[:, n * HD:n * HD + HD].astype(BF), pn[h], (((0,), (0,)), ((), ())),
                preferred_element_type=F32,
            )
            o = o.T
            for g in range(4):
                of[4 * h + g] = o[g * TOK:g * TOK + TOK, :]
        for r in range(ROWS):
            for n in range(8 * (j - 4), 8 * (j - 3)):
                outv[r, :, n * HD:n * HD + HD] = of[n, pl.ds(r, STEPS, stride=16), :].astype(BF)
        cols = pl.ds((j - 4) * 1024, 1024)
        lo_.append(local(outv.at[:, :, cols], out.at[:, :, cols]))

    tpad[...] = jnp.zeros_like(tpad)
    gT[GR:, :] = jnp.zeros((GP - GR, 128), F32)
    mine = pl.multiple_of(c * GH, GH)
    theirs = pl.multiple_of((1 - c) * GH, GH)
    for cp in lg:
        cp.wait()
    transposed(gT, gav, gbv, -rate_a, -rate_b)
    g1s[0:GH, :] = gT[pl.ds(theirs, GH), :].astype(BF)
    bmine = pl.ds(pl.multiple_of(DS + c * 32, 32), 32)
    btheirs = pl.ds(pl.multiple_of(DS + (1 - c) * 32, 32), 32)
    g1s[GH:, :] = gT[btheirs, :].astype(BF)
    lw[1].wait()
    lw[2].wait()
    pl.semaphore_wait(barrier, len(peers))

    g1 = remote(g1s, g1r, sib)
    w1 = [weight(1, 0, 80, part), weight(1, 80, 80, other)]
    w2 = weight(2, 0, 160, other)
    for cp in lh:
        cp.wait()
    pick(1 - a, hsend)
    hr = [hidden(i) for i in range(5)]
    pick(a, hown)
    lw[0].wait()
    product(0, 0, TOK)
    stage(0, 0)

    g1.wait_recv()
    h2[...] = (gT[pl.ds(mine, GH), :] + g1r[0:GH, :].astype(F32)).astype(BF)
    g3 = []
    for i in range(1, NZ):
        rows = pl.ds(pl.multiple_of(lax.rem(z + i, NZ) * GZ, GZ), GZ)
        g3.append(remote(h2.at[rows, :], g3r.at[i], zpeer[i]))
    product(0, TOK, 7 * TOK)
    for cp in lf:
        cp.wait()
    fT[GR:, :] = jnp.zeros((GP - GR, 128), F32)
    transposed(fT, fav, fbv, 0.5, 0.5)
    hball[y] = (
        gT[bmine, :] + g1r[GH:, :].astype(F32) + fT[bmine, :] * 0.125
    ).astype(BF)
    b0 = [remote(hball.at[y], hball.at[y], ypeer[i]) for i in range(1, NY)]
    stage(0, 1)

    for cp in w1:
        cp.wait_recv()
    f1 = forward(1)
    lw[3].wait()
    w3 = weight(3, 0, 160, other)
    lw[4].wait()
    w4 = [weight(4, 0, 80, part)]
    hr += [hidden(i) for i in range(5, 8)]
    w4.append(weight(4, 80, 80, other))
    prepare_masks()
    hr[0].wait_recv()
    f1.wait_recv()
    product(1, 0, TOK)
    stage(1, 0)
    for i in (1, 2):
        hr[i].wait_recv()
    product(1, TOK, 2 * TOK)
    w2.wait_recv()
    f2 = forward(2)
    stage(0, 2)

    piece = pl.ds(pl.multiple_of(c * GH + z * GZ, GZ), GZ)
    total = h2[pl.ds(pl.multiple_of(z * GZ, GZ), GZ), :].astype(F32) + fT[piece, :]
    for i in range(1, NZ):
        g3[i - 1].wait_recv()
        total = total + g3r[i].astype(F32)
    g2s[...] = total
    g2 = [remote(g2s, g2r.at[i], device) for i, device in enumerate((xflip, part, other))]
    for cp in b0:
        cp.wait_recv()
    b3 = [
        remote(hball.at[lax.rem(z + i, NZ)], b3r.at[i], zpeer[i]) for i in range(1, NZ)
    ]

    f2.wait_recv()
    product(2, 0, TOK)
    stage(2, 0)
    stage(1, 1)
    prepare_queries()
    kc[16 * ROWS:, :] = jnp.zeros((16, 1024), BF)
    vc[16 * ROWS:, :] = jnp.zeros((16, 1024), BF)
    for i in (3, 4):
        hr[i].wait_recv()
    product(2, TOK, 4 * TOK)
    w3.wait_recv()
    f3 = forward(3)
    stage(0, 3)
    product(1, 3 * TOK, 2 * TOK)
    f3.wait_recv()
    product(3, 0, TOK)
    stage(3, 0)

    for cp in g2:
        cp.wait_recv()
    tot[c, z, a] = (g2s[...] + g2r[0]).astype(BF)
    tot[c, z, 1 - a] = (g2r[1] + g2r[2]).astype(BF)
    g4 = [remote(tot.at[c, z], tot.at[c, z], zpeer[i]) for i in range(1, NZ)]

    stage(2, 1)
    stage(1, 2)
    for cp in w4:
        cp.wait_recv()
    f4 = forward(4)
    lk.wait()
    lv.wait()
    total = last(0)
    xs[...] = total[:, 256:512].astype(BF)
    x0 = remote(xs, xr, part)
    first[...] = total[:, 0:256]
    total = hball[z].astype(F32)
    for i in range(1, NZ):
        b3[i - 1].wait_recv()
        total = total + b3r[i].astype(F32)
    b2s[...] = total
    b2 = [remote(b2s, b2r.at[i], device) for i, device in enumerate((xflip, part, other))]
    product(3, TOK, 4 * TOK)
    f4.wait_recv()
    product(4, 0, TOK)
    stage(4, 0)
    stage(3, 1)
    for cp in g4:
        cp.wait_recv()
    g5 = remote(tot.at[c], tot.at[c], sib)
    for i in (5, 6, 7):
        hr[i].wait_recv()
    product(2, 5 * TOK, 3 * TOK)
    stage(2, 2)
    g5.wait_recv()

    def new_a(side):
        return jnp.concatenate([tot[e // NZ, e % NZ, side] for e in range(10)], axis=0)

    pu[...] = jnp.dot(hown[...], new_a(a), preferred_element_type=F32) + jnp.dot(
        hrem[...], new_a(1 - a), preferred_element_type=F32
    )
    ustage(0)
    for cp in b2:
        cp.wait_recv()
    nball[c, z, a] = (b2s[...] + b2r[0]).astype(BF)
    nball[c, z, 1 - a] = (b2r[1] + b2r[2]).astype(BF)
    b4 = [remote(nball.at[c, z], nball.at[c, z], zpeer[i]) for i in range(1, NZ)]
    product(1, 5 * TOK, 3 * TOK)
    stage(1, 3)
    product(4, TOK, 7 * TOK)
    stage(4, 1)
    ustage(1)
    product(3, 5 * TOK, 3 * TOK)
    stage(3, 2)
    cached(0)
    stage(2, 3)
    cached(1)

    ustage(2)
    stage(4, 2)
    ustage(3)
    stage(3, 3)
    for cp in b4:
        cp.wait_recv()
    b5 = remote(nball.at[c], nball.at[c], sib)
    cached(2)
    stage(4, 3)
    cached(3)
    for h in range(4, KVH):
        cached(h)
    prepare_rotation()
    back = jnp.concatenate([tot[e // NZ, e % NZ, a].astype(F32) for e in range(12)], axis=0).T
    nav[...] = back[:, 0:DS]
    lo_ += [local(nav, na)]

    u = pu[7 * TOK:, :]
    for way in range(2):
        usent[3, way].wait_recv()
        u = u + rbu[3, way].astype(F32)
    u = u * 0.25
    lane = lax.broadcasted_iota(jnp.int32, u.shape, 1)
    us = [jnp.where(lane >> 6 == p, u, 0.0).astype(BF) for p in range(2)]
    x0.wait_recv()
    b5.wait_recv()
    back = jnp.concatenate(
        [nball[0, y, a].astype(F32), nball[1, y, a].astype(F32), jnp.zeros((64, 128), F32)], axis=0
    ).T
    nbv[...] = back[:, 0:R]
    lo_ += [local(nbv, nb)]
    allb = [
        jnp.concatenate([nball[core, i, side] for i in range(NY) for core in range(2)], axis=0)
        for side in range(2)
    ]
    new_keys(0, first[...] + xr[...].astype(F32) + adapter(0))
    for k in range(1, NC):
        total = last(k)
        for n, j in enumerate(PIECES[k]):
            x = total[:, n * 256:n * 256 + 256] + adapter(j)
            if j < 4:
                new_keys(j, x)
            else:
                new_values(j, x)
    assert count[0] == N_REMOTE and nloc[0] == N_LOCAL
    for cp in lo_:
        cp.wait()
    for cp in started:
        cp.wait_send()


N_LOCAL = 22
N_REMOTE = 6 + 4 + 8 + 40 + 7 + 1 + 7 + 3 + 7 + 1 + 1 + 7 + 7 + 3 + 7 + 1


def transfers(rate_a, rate_b, *operands):
    def body(*refs):
        transfer_kernel(rate_a, rate_b, *refs)

    vmem = pl.BlockSpec(memory_space=pltpu.VMEM)
    hbm = pl.BlockSpec(memory_space=pltpu.HBM)
    smem = pl.BlockSpec(memory_space=pltpu.SMEM)
    return pl.pallas_call(
        body,
        out_shape=(
            jax.ShapeDtypeStruct((ROWS, STEPS, QH * HD), BF),
            jax.ShapeDtypeStruct((2 * R, DS), F32),
            jax.ShapeDtypeStruct((2 * R, R), F32),
        ),
        in_specs=[hbm] * 6 + [vmem, hbm, hbm, hbm, smem, smem],
        out_specs=(hbm, hbm, hbm),
        scratch_shapes=[
            pltpu.VMEM((STEPS, DS, 16 * ROWS), BF),
            pltpu.VMEM((8 * TOK, DS), BF),
            pltpu.VMEM((8 * TOK, DS), BF),
            pltpu.VMEM((8 * TOK, DS), BF),
            pltpu.VMEM((DS, 256), BF),
            pltpu.VMEM((3, DS, 512), BF),
            pltpu.VMEM((3, DS, 512), BF),
            pltpu.VMEM((DS, 256), BF),
            pltpu.VMEM((DS, 256), BF),
            pltpu.VMEM((4, 8 * TOK, 512), F32),
            pltpu.VMEM((8 * TOK, 256), F32),
            pltpu.VMEM((4, 2, TOK, 256), BF),
            pltpu.VMEM((4, 2, TOK, 256), BF),
            pltpu.VMEM((4, 3, 2, TOK, 512), BF),
            pltpu.VMEM((4, 3, 2, TOK, 512), BF),
            pltpu.VMEM((2, TOK, 128), BF),
            pltpu.VMEM((2, TOK, 128), BF),
            pltpu.VMEM((3, 2, TOK, 256), BF),
            pltpu.VMEM((3, 2, TOK, 256), BF),
            pltpu.VMEM((TOK, 256), F32),
            pltpu.VMEM((TOK, 256), BF),
            pltpu.VMEM((TOK, 256), BF),
            pltpu.VMEM((8 * TOK, 128), F32),
            pltpu.VMEM((4, 2, TOK, 128), BF),
            pltpu.VMEM((4, 2, TOK, 128), BF),
            pltpu.VMEM((2 * R, DS), F32),
            pltpu.VMEM((2 * R, R), F32),
            pltpu.VMEM((2 * R, DS), F32),
            pltpu.VMEM((2 * R, R), F32),
            pltpu.VMEM((128, GR), F32),
            pltpu.VMEM((GP, 128), F32),
            pltpu.VMEM((GP, 128), F32),
            pltpu.VMEM((GH + 32, 128), BF),
            pltpu.VMEM((GH + 32, 128), BF),
            pltpu.VMEM((GH, 128), BF),
            pltpu.VMEM((NZ, GZ, 128), BF),
            pltpu.VMEM((GZ, 128), F32),
            pltpu.VMEM((3, GZ, 128), F32),
            pltpu.VMEM((2, NZ, 2, GZ, 128), BF),
            pltpu.VMEM((2, NY, 2, 32, 128), BF),
            pltpu.VMEM((NY, 32, 128), BF),
            pltpu.VMEM((NZ, 32, 128), BF),
            pltpu.VMEM((32, 128), F32),
            pltpu.VMEM((3, 32, 128), F32),
            pltpu.VMEM((ROWS, STEPS, QH * HD), BF),
            pltpu.VMEM((QH, TOK, HD), F32),
            pltpu.VMEM((KVH, 256, HD), BF),
            pltpu.VMEM((256, 1024), BF),
            pltpu.VMEM((256, 1024), BF),
            pltpu.VMEM((256, 256), F32),
            pltpu.VMEM((TOK, 256), F32),
            pltpu.VMEM((TOK, HD), F32),
            pltpu.VMEM((TOK, HD), F32),
            pltpu.VMEM((KVH, 1, 256), F32),
            pltpu.VMEM((KVH, 1, 256), F32),
            pltpu.VMEM((KVH, HD, 256), F32),
            pltpu.VMEM((KVH, TOK, 256), BF),
            pltpu.VMEM((QH, TOK, HD), F32),
            pltpu.VMEM((ROWS, STEPS, QH * HD), BF),
            pltpu.VMEM((2 * R, DS), F32),
            pltpu.VMEM((2 * R, R), F32),
            pltpu.SemaphoreType.DMA((N_LOCAL,)),
            pltpu.SemaphoreType.DMA((N_REMOTE,)),
            pltpu.SemaphoreType.DMA((N_REMOTE,)),
        ],
        compiler_params=pltpu.CompilerParams(
            collective_id=0, has_side_effects=True, vmem_limit_bytes=56 * 1024 * 1024
        ),
    )(*operands)


def results_kernel(att, na, nb, att_out, na_out, nb_out, attv, nav, nbv, sem):
    parts = [(att.at[pl.ds(3 * i, 3)], attv.at[pl.ds(3 * i, 3)], att_out.at[pl.ds(3 * i, 3)])
             for i in range(5)]
    parts += [(na, nav, na_out), (nb, nbv, nb_out)]
    reads = [pltpu.make_async_copy(x, v, sem.at[0, i]) for i, (x, v, _) in enumerate(parts)]
    writes = [pltpu.make_async_copy(v, o, sem.at[1, i]) for i, (_, v, o) in enumerate(parts)]
    for cp in reads:
        cp.start()
    for read, write in zip(reads, writes):
        read.wait()
        write.start()
    for cp in writes:
        cp.wait()


def results(*operands):
    hbm = pl.BlockSpec(memory_space=pltpu.HBM)
    return pl.pallas_call(
        results_kernel,
        out_shape=tuple(jax.ShapeDtypeStruct(x.shape, x.dtype) for x in operands),
        in_specs=[hbm] * 3,
        out_specs=(hbm,) * 3,
        scratch_shapes=[pltpu.VMEM(x.shape, x.dtype) for x in operands]
        + [pltpu.SemaphoreType.DMA((2, 7))],
        compiler_params=pltpu.CompilerParams(vmem_limit_bytes=56 * 1024 * 1024),
    )(*operands)


def per_device(
    hidden_in, kv_weight, factor_a, factor_b, grad_a, grad_b, key_gain,
    queries, cache_keys, cache_values, cache_lengths, positions,
):
    groups_dp = lax.axis_size("dp")
    rate_a = 2.0 / math.sqrt(groups_dp * D)
    rate_b = 2.0 / math.sqrt(groups_dp * R)
    attended, na, nb = results(*transfers(
        rate_a, rate_b, hidden_in.transpose(1, 2, 0), kv_weight,
        grad_a.reshape(2 * R, DS), grad_b.reshape(2 * R, R),
        factor_a.reshape(2 * R, DS), factor_b.reshape(2 * R, R),
        key_gain.reshape(1, HD), queries,
        cache_keys.reshape(16 * ROWS, KVH * HD), cache_values.reshape(16 * ROWS, KVH * HD),
        cache_lengths, positions,
    ))
    return (attended, na.reshape(2, R, DS), nb.reshape(2, R, R))


def solution(mesh):
    return jax.shard_map(
        per_device,
        mesh=mesh,
        in_specs=(
            P("dp", None, "tensor"),
            P(None, "tensor", None),
            P(None, None, "tensor"),
            P(None, None, "tensor"),
            P("dp", None, None, "tensor"),
            P("dp", None, None, "tensor"),
            P(),
            P(("dp", "tensor"), None, None),
            P(("dp", "tensor"), None, None),
            P(("dp", "tensor"), None, None),
            P(("dp", "tensor")),
            P(("dp", "tensor")),
        ),
        out_specs=(
            P(("dp", "tensor"), None, None),
            P(None, None, "tensor"),
            P(None, None, "tensor"),
        ),
        check_vma=False,
    )
```

```python
import math

import jax
import jax.numpy as jnp
from jax import lax
from jax.experimental import pallas as pl
from jax.experimental.pallas import tpu as pltpu
from jax.sharding import PartitionSpec as P

D = 5120
KVH = 8
HD = 128
QH = 32
R = 64
STEPS = 4
KV = 2048
MESH = pl.DeviceIdType.MESH

NY = 8
NZ = 8
TOK = 64
DS = 320
ORDER = (4, 3, 5, 2, 6, 1, 7, 0)
NC = 5
WIDTH = (512, 256, 512, 512, 512)
PIECES = ((0,), (1,), (2, 3), (4, 5), (6, 7))
GR = 384
GP = 512
GH = GP // 2
GZ = GH // NZ
ROWS = 15
SCALE = HD ** -0.5
NEG = -1e30
F32 = jnp.float32
BF = jnp.bfloat16


def transfer_kernel(
    rate_a, rate_b,
    hT, kv, ga, gb, fa, fb, gain, q, ck, cv, lens, pos,
    out, na, nb,
    hin, hsend, hown, hrem, wfirst, wown, wrem, wnarrow, wnarrowr,
    pk, pknarrow, sb0, rb0, sb, rb, sb0l, rb0l, sbl, rbl, first, xs, xr,
    pu, sbu, rbu,
    gav, gbv, fav, fbv, tpad, gT, fT, g1s, g1r, h2, g3r, g2s, g2r, tot, nball, hball, b3r, b2s, b2r,
    qin, qs, qh, kc, vc, biasc, biasn, cost, sint, mc, lc, oc, pn, of, outv, nav, nbv,
    loc, ssem, rsem,
):
    dp = lax.axis_index("dp")
    tn = lax.axis_index("tensor")
    xh, z, c = dp // 16, lax.rem(dp // 2, 8), lax.rem(dp, 2)
    a, y = tn // NY, lax.rem(tn, NY)
    dflip = lax.rem(dp + 16, 32)
    tflip = lax.rem(tn + 8, 16)
    sib = (dp + 1 - 2 * c, tn)
    xflip = (dflip, tn)
    part = (dp, tflip)
    other = (dflip, tflip)
    ypeer = [None] + [(dp, a * NY + lax.rem(y + i, NY)) for i in range(1, NY)]
    zpeer = [None] + [(xh * 16 + lax.rem(z + i, NZ) * 2 + c, tn) for i in range(1, NZ)]
    ring = (ypeer[1], ypeer[NY - 1])
    peers = [sib, xflip, part, other] + ypeer[1:] + zpeer[1:]

    barrier = pltpu.get_barrier_semaphore()
    for peer in peers:
        pl.semaphore_signal(barrier, inc=1, device_id=peer, device_id_type=MESH)

    nloc = [0]

    def local(src, dst):
        cp = pltpu.make_async_copy(src, dst, loc.at[nloc[0]])
        nloc[0] += 1
        cp.start()
        return cp

    lh = [local(hT.at[t], hin.at[t]) for t in range(STEPS)]
    lw = [local(kv.at[0, :, pl.ds(0, 256)], wfirst), local(kv.at[0, :, pl.ds(256, 256)], wnarrow)]
    lg = [local(ga, gav), local(gb, gbv)]
    lw += [
        local(kv.at[0, :, pl.ds(512, 512)], wown.at[0]),
        local(kv.at[1, :, pl.ds(0, 512)], wown.at[1]),
        local(kv.at[1, :, pl.ds(512, 512)], wown.at[2]),
    ]
    lq = local(q, qin)
    lk = local(ck, kc.at[pl.ds(0, 16 * ROWS)])
    lv = local(cv, vc.at[pl.ds(0, 16 * ROWS)])
    lf = [local(fa, fav), local(fb, fbv)]

    count = [0]
    started = []

    def remote(src, dst, device):
        i = count[0]
        count[0] += 1
        cp = pltpu.make_async_remote_copy(
            src_ref=src, dst_ref=dst, send_sem=ssem.at[i], recv_sem=rsem.at[i],
            device_id=device, device_id_type=MESH,
        )
        cp.start()
        started.append(cp)
        return cp

    def transposed(into, wide, narrow, by_a, by_b):
        tpad[:, 0:DS] = wide[...] * by_a
        into[0:GR, :] = tpad[...].T
        tpad[:, 0:R] = narrow[...] * by_b
        into[DS:GR, :] = tpad[:, 0:128].T[0:R, :]

    def pick(side, into):
        row = lax.broadcasted_iota(jnp.int32, (128, 16 * ROWS), 0)
        col = lax.broadcasted_iota(jnp.int32, (128, 16 * ROWS), 1)
        target = jnp.zeros((128, 16 * ROWS), jnp.int32)
        for i, j in enumerate(ORDER):
            first = (side * NY + lax.rem(y + j, NY)) * ROWS
            target = jnp.where(row >> 4 == i, first + (row & 15), target)
        sel = jnp.where((col == target) & ((row & 15) < ROWS), 1.0, 0.0).astype(BF)
        for t in range(STEPS):
            x = lax.dot_general(
                sel, hin[t], (((1,), (1,)), ((), ())), preferred_element_type=F32
            ).astype(BF)
            for i in range(8):
                into[i * TOK + 16 * t:i * TOK + 16 * t + 16, :] = x[16 * i:16 * i + 16, :]

    wo = (None, wnarrow, wown.at[0], wown.at[1], wown.at[2])
    wr = (None, wnarrowr, wrem.at[0], wrem.at[1], wrem.at[2])
    krow = c * (DS // 2)

    def weight(k, lo, n, device):
        rows = pl.ds(pl.multiple_of(krow + lo, 16), n)
        return remote(wo[k].at[rows], wr[k].at[rows], device)

    def forward(k):
        ref = wr[k].at[pl.ds(pl.multiple_of(krow, 16), DS // 2)]
        return remote(ref, ref, sib)

    def hidden(i):
        rows = pl.ds(i * TOK, TOK)
        return remote(hsend.at[rows], hrem.at[rows], part)

    pks = [pk.at[0], pknarrow, pk.at[1], pk.at[2], pk.at[3]]

    def product(k, lo, n):
        rows = slice(lo, lo + n)
        if k == 0:
            pk[0, rows, 0:256] = jnp.dot(hown[rows, :], wfirst[...], preferred_element_type=F32)
            pk[0, rows, 256:512] = jnp.dot(hsend[rows, :], wfirst[...], preferred_element_type=F32)
            return
        pks[k][rows, :] = jnp.dot(
            hown[rows, :], wo[k][...], preferred_element_type=F32
        ) + jnp.dot(hrem[rows, :], wr[k][...], preferred_element_type=F32)

    def slot(k, s, way):
        n = max(k - 1, 0)
        if s == 0:
            return (sb0l.at[way], rb0l.at[way]) if k == 1 else (sb0.at[n, way], rb0.at[n, way])
        if k == 1:
            return sbl.at[s - 1, way], rbl.at[s - 1, way]
        return sb.at[n, s - 1, way], rb.at[n, s - 1, way]

    sent = {}

    def stage(k, s):
        half = WIDTH[k] // 2
        for way in range(2):
            src, dst = slot(k, s, way)
            cut = slice(way * half, way * half + half)
            rest = slice((1 - way) * half, (1 - way) * half + half)
            if s == 0:
                src[...] = pks[k][0:TOK, cut].astype(BF)
            else:
                rows = slice((2 * s - 1 + way) * TOK, (2 * s + way) * TOK)
                sent[k, s - 1, way].wait_recv()
                got = slot(k, s - 1, way)[1]
                if s == 1:
                    src[:, cut] = (pks[k][rows, cut] + got[...].astype(F32)).astype(BF)
                    src[:, rest] = pks[k][rows, rest].astype(BF)
                else:
                    src[...] = (pks[k][rows, :] + got[...].astype(F32)).astype(BF)
            sent[k, s, way] = remote(src, dst, ring[way])

    def last(k):
        total = pks[k][7 * TOK:8 * TOK, :]
        for way in range(2):
            sent[k, 3, way].wait_recv()
            total = total + slot(k, 3, way)[1][...].astype(F32)
        return total

    def adapter(j):
        return lax.dot_general(
            us[j // 4], allb[(j % 4) // 2][(j % 2) * 256:(j % 2) * 256 + 256],
            (((1,), (1,)), ((), ())), preferred_element_type=F32,
        )

    usent = {}

    def ustage(s):
        if s == 0:
            sbu[0, 0] = pu[0:TOK, :].astype(BF)
            usent[0, 0] = remote(sbu.at[0, 0], rbu.at[0, 0], ring[0])
            return
        for way in range(2):
            total = pu[(2 * s - 1 + way) * TOK:(2 * s + way) * TOK, :]
            if s > 1 or way == 0:
                usent[s - 1, way].wait_recv()
                total = total + rbu[s - 1, way].astype(F32)
            sbu[s, way] = total.astype(BF)
            usent[s, way] = remote(sbu.at[s, way], rbu.at[s, way], ring[way])

    def prepare_masks():
        j = lax.broadcasted_iota(jnp.int32, (256, 256), 0)
        i = lax.broadcasted_iota(jnp.int32, (256, 256), 1)
        length = jnp.zeros((256, 256), jnp.int32)
        for r in range(ROWS):
            length = jnp.where(j >> 4 == r, lens[r], length)
        ok = ((i & 15) == (j >> 4)) & ((j & 15) < length)
        biasc[...] = jnp.where(ok, 0.0, NEG)
        j = lax.broadcasted_iota(jnp.int32, (TOK, 256), 0)
        i = lax.broadcasted_iota(jnp.int32, (TOK, 256), 1)
        ok = ((i & 15) == (j & 15)) & (((i >> 4) & 3) >= (j >> 4))
        biasn[...] = jnp.where(ok, 0.0, NEG)

    def prepare_rotation():
        row = lax.broadcasted_iota(jnp.int32, (16, HD), 0)
        place = jnp.zeros((16, HD), jnp.int32)
        for r in range(ROWS):
            place = jnp.where(row == r, pos[r], place)
        lane = lax.broadcasted_iota(jnp.int32, (16, HD), 1)
        i = lane & 63
        coarse = jnp.zeros((16, HD), F32)
        fine = jnp.zeros((16, HD), F32)
        for n in range(8):
            coarse = jnp.where(i >> 3 == n, 1000000.0 ** (-16.0 * n / HD), coarse)
            fine = jnp.where((i & 7) == n, 1000000.0 ** (-2.0 * n / HD), fine)
        freq = coarse * fine
        sign = jnp.where(lane < 64, -1.0, 1.0)
        for t in range(STEPS):
            angle = (place + t).astype(F32) * freq
            cost[16 * t:16 * t + 16, :] = jnp.cos(angle)
            sint[16 * t:16 * t + 16, :] = jnp.sin(angle) * sign

    def prepare_queries():
        lq.wait()
        qs[...] = jnp.zeros_like(qs)
        for r in range(ROWS):
            row = qin[r].astype(F32)
            for n in range(QH):
                qs[n, pl.ds(r, STEPS, stride=16), :] = row[:, n * HD:n * HD + HD]
        for h in range(KVH):
            for g in range(4):
                qh[h, g * TOK:g * TOK + TOK, :] = qs[4 * h + g].astype(BF)

    def cached(h):
        cols = slice(h * HD, h * HD + HD)
        s = lax.dot_general(
            kc[:, cols], qh[h], (((1,), (1,)), ((), ())), preferred_element_type=F32
        ) * SCALE + biasc[...]
        top = jnp.max(s, axis=0, keepdims=True)
        e = jnp.exp(s - top)
        mc[h] = top
        lc[h] = jnp.sum(e, axis=0, keepdims=True)
        oc[h] = lax.dot_general(
            vc[:, cols], e.astype(BF), (((0,), (0,)), ((), ())), preferred_element_type=F32
        )

    def new_keys(j, x):
        for n in range(2):
            h = 2 * j + n
            v = x[:, n * HD:n * HD + HD]
            v = v * lax.rsqrt(jnp.mean(v * v, axis=-1, keepdims=True) + 1e-06) * gain[...]
            turned = jnp.concatenate([v[:, 64:], v[:, :64]], axis=-1)
            key = (v * cost[...] + turned * sint[...]).astype(BF)
            s = lax.dot_general(
                key, qh[h], (((1,), (1,)), ((), ())), preferred_element_type=F32
            ) * SCALE + biasn[...]
            top = jnp.maximum(mc[h], jnp.max(s, axis=0, keepdims=True))
            e = jnp.exp(s - top)
            back = jnp.exp(mc[h] - top)
            inv = 1.0 / (back * lc[h] + jnp.sum(e, axis=0, keepdims=True))
            pn[h] = (e * inv).astype(BF)
            oc[h] = oc[h] * (back * inv)

    lo_ = []

    def new_values(j, x):
        for n in range(2):
            h = 2 * (j - 4) + n
            o = oc[h] + lax.dot_general(
                x[:, n * HD:n * HD + HD].astype(BF), pn[h], (((0,), (0,)), ((), ())),
                preferred_element_type=F32,
            )
            o = o.T
            for g in range(4):
                of[4 * h + g] = o[g * TOK:g * TOK + TOK, :]
        for r in range(ROWS):
            for n in range(8 * (j - 4), 8 * (j - 3)):
                outv[r, :, n * HD:n * HD + HD] = of[n, pl.ds(r, STEPS, stride=16), :].astype(BF)
        cols = pl.ds((j - 4) * 1024, 1024)
        lo_.append(local(outv.at[:, :, cols], out.at[:, :, cols]))

    tpad[...] = jnp.zeros_like(tpad)
    gT[GR:, :] = jnp.zeros((GP - GR, 128), F32)
    mine = pl.multiple_of(c * GH, GH)
    theirs = pl.multiple_of((1 - c) * GH, GH)
    for cp in lg:
        cp.wait()
    transposed(gT, gav, gbv, -rate_a, -rate_b)
    g1s[0:GH, :] = gT[pl.ds(theirs, GH), :].astype(BF)
    bmine = pl.ds(pl.multiple_of(DS + c * 32, 32), 32)
    btheirs = pl.ds(pl.multiple_of(DS + (1 - c) * 32, 32), 32)
    g1s[GH:, :] = gT[btheirs, :].astype(BF)
    lw[1].wait()
    lw[2].wait()
    pl.semaphore_wait(barrier, len(peers))

    g1 = remote(g1s, g1r, sib)
    w1 = [weight(1, 0, 80, part), weight(1, 80, 80, other)]
    w2 = weight(2, 0, 160, other)
    for cp in lh:
        cp.wait()
    pick(1 - a, hsend)
    hr = [hidden(i) for i in range(5)]
    pick(a, hown)
    lw[0].wait()
    product(0, 0, TOK)
    stage(0, 0)

    g1.wait_recv()
    h2[...] = (gT[pl.ds(mine, GH), :] + g1r[0:GH, :].astype(F32)).astype(BF)
    g3 = []
    for i in range(1, NZ):
        rows = pl.ds(pl.multiple_of(lax.rem(z + i, NZ) * GZ, GZ), GZ)
        g3.append(remote(h2.at[rows, :], g3r.at[i], zpeer[i]))
    product(0, TOK, 7 * TOK)
    for cp in lf:
        cp.wait()
    fT[GR:, :] = jnp.zeros((GP - GR, 128), F32)
    transposed(fT, fav, fbv, 0.5, 0.5)
    hball[y] = (
        gT[bmine, :] + g1r[GH:, :].astype(F32) + fT[bmine, :] * 0.125
    ).astype(BF)
    b0 = [remote(hball.at[y], hball.at[y], ypeer[i]) for i in range(1, NY)]
    stage(0, 1)

    for cp in w1:
        cp.wait_recv()
    f1 = forward(1)
    lw[3].wait()
    w3 = weight(3, 0, 160, other)
    lw[4].wait()
    w4 = [weight(4, 0, 80, part)]
    hr += [hidden(i) for i in range(5, 8)]
    w4.append(weight(4, 80, 80, other))
    prepare_masks()
    hr[0].wait_recv()
    f1.wait_recv()
    product(1, 0, TOK)
    stage(1, 0)
    for i in (1, 2):
        hr[i].wait_recv()
    product(1, TOK, 2 * TOK)
    w2.wait_recv()
    f2 = forward(2)
    stage(0, 2)

    piece = pl.ds(pl.multiple_of(c * GH + z * GZ, GZ), GZ)
    total = h2[pl.ds(pl.multiple_of(z * GZ, GZ), GZ), :].astype(F32) + fT[piece, :]
    for i in range(1, NZ):
        g3[i - 1].wait_recv()
        total = total + g3r[i].astype(F32)
    g2s[...] = total
    g2 = [remote(g2s, g2r.at[i], device) for i, device in enumerate((xflip, part, other))]
    for cp in b0:
        cp.wait_recv()
    b3 = [
        remote(hball.at[lax.rem(z + i, NZ)], b3r.at[i], zpeer[i]) for i in range(1, NZ)
    ]

    f2.wait_recv()
    product(2, 0, TOK)
    stage(2, 0)
    stage(1, 1)
    prepare_queries()
    kc[16 * ROWS:, :] = jnp.zeros((16, 1024), BF)
    vc[16 * ROWS:, :] = jnp.zeros((16, 1024), BF)
    for i in (3, 4):
        hr[i].wait_recv()
    product(2, TOK, 4 * TOK)
    w3.wait_recv()
    f3 = forward(3)
    stage(0, 3)
    product(1, 3 * TOK, 2 * TOK)
    f3.wait_recv()
    product(3, 0, TOK)
    stage(3, 0)

    for cp in g2:
        cp.wait_recv()
    tot[c, z, a] = (g2s[...] + g2r[0]).astype(BF)
    tot[c, z, 1 - a] = (g2r[1] + g2r[2]).astype(BF)
    g4 = [remote(tot.at[c, z], tot.at[c, z], zpeer[i]) for i in range(1, NZ)]

    stage(2, 1)
    stage(1, 2)
    for cp in w4:
        cp.wait_recv()
    f4 = forward(4)
    lk.wait()
    lv.wait()
    total = last(0)
    xs[...] = total[:, 256:512].astype(BF)
    x0 = remote(xs, xr, part)
    first[...] = total[:, 0:256]
    total = hball[z].astype(F32)
    for i in range(1, NZ):
        b3[i - 1].wait_recv()
        total = total + b3r[i].astype(F32)
    b2s[...] = total
    b2 = [remote(b2s, b2r.at[i], device) for i, device in enumerate((xflip, part, other))]
    product(3, TOK, 4 * TOK)
    f4.wait_recv()
    product(4, 0, TOK)
    stage(4, 0)
    stage(3, 1)
    for cp in g4:
        cp.wait_recv()
    g5 = remote(tot.at[c], tot.at[c], sib)
    for i in (5, 6, 7):
        hr[i].wait_recv()
    product(2, 5 * TOK, 3 * TOK)
    stage(2, 2)
    g5.wait_recv()

    def new_a(side):
        return jnp.concatenate([tot[e // NZ, e % NZ, side] for e in range(10)], axis=0)

    pu[...] = jnp.dot(hown[...], new_a(a), preferred_element_type=F32) + jnp.dot(
        hrem[...], new_a(1 - a), preferred_element_type=F32
    )
    ustage(0)
    for cp in b2:
        cp.wait_recv()
    nball[c, z, a] = (b2s[...] + b2r[0]).astype(BF)
    nball[c, z, 1 - a] = (b2r[1] + b2r[2]).astype(BF)
    b4 = [remote(nball.at[c, z], nball.at[c, z], zpeer[i]) for i in range(1, NZ)]
    product(1, 5 * TOK, 3 * TOK)
    stage(1, 3)
    product(4, TOK, 7 * TOK)
    stage(4, 1)
    ustage(1)
    product(3, 5 * TOK, 3 * TOK)
    stage(3, 2)
    cached(0)
    stage(2, 3)
    cached(1)

    ustage(2)
    stage(4, 2)
    ustage(3)
    stage(3, 3)
    for cp in b4:
        cp.wait_recv()
    b5 = remote(nball.at[c], nball.at[c], sib)
    cached(2)
    stage(4, 3)
    cached(3)
    for h in range(4, KVH):
        cached(h)
    prepare_rotation()
    back = jnp.concatenate([tot[e // NZ, e % NZ, a].astype(F32) for e in range(12)], axis=0).T
    nav[...] = back[:, 0:DS]
    lo_ += [local(nav, na)]

    u = pu[7 * TOK:, :]
    for way in range(2):
        usent[3, way].wait_recv()
        u = u + rbu[3, way].astype(F32)
    u = u * 0.25
    lane = lax.broadcasted_iota(jnp.int32, u.shape, 1)
    us = [jnp.where(lane >> 6 == p, u, 0.0).astype(BF) for p in range(2)]
    x0.wait_recv()
    b5.wait_recv()
    allb = [
        jnp.concatenate([nball[core, i, side] for i in range(NY) for core in range(2)], axis=0)
        for side in range(2)
    ]
    new_keys(0, first[...] + xr[...].astype(F32) + adapter(0))
    for k in range(1, NC):
        if k == 3:
            back = jnp.concatenate(
                [nball[0, y, a].astype(F32), nball[1, y, a].astype(F32), jnp.zeros((64, 128), F32)], axis=0
            ).T
            nbv[...] = back[:, 0:R]
            lo_ += [local(nbv, nb)]
        total = last(k)
        for n, j in enumerate(PIECES[k]):
            x = total[:, n * 256:n * 256 + 256] + adapter(j)
            if j < 4:
                new_keys(j, x)
            else:
                new_values(j, x)
    assert count[0] == N_REMOTE and nloc[0] == N_LOCAL
    for cp in lo_:
        cp.wait()
    for cp in started:
        cp.wait_send()


N_LOCAL = 22
N_REMOTE = 6 + 4 + 8 + 40 + 7 + 1 + 7 + 3 + 7 + 1 + 1 + 7 + 7 + 3 + 7 + 1


def transfers(rate_a, rate_b, *operands):
    def body(*refs):
        transfer_kernel(rate_a, rate_b, *refs)

    vmem = pl.BlockSpec(memory_space=pltpu.VMEM)
    hbm = pl.BlockSpec(memory_space=pltpu.HBM)
    smem = pl.BlockSpec(memory_space=pltpu.SMEM)
    return pl.pallas_call(
        body,
        out_shape=(
            jax.ShapeDtypeStruct((ROWS, STEPS, QH * HD), BF),
            jax.ShapeDtypeStruct((2 * R, DS), F32),
            jax.ShapeDtypeStruct((2 * R, R), F32),
        ),
        in_specs=[hbm] * 6 + [vmem, hbm, hbm, hbm, smem, smem],
        out_specs=(hbm, hbm, hbm),
        scratch_shapes=[
            pltpu.VMEM((STEPS, DS, 16 * ROWS), BF),
            pltpu.VMEM((8 * TOK, DS), BF),
            pltpu.VMEM((8 * TOK, DS), BF),
            pltpu.VMEM((8 * TOK, DS), BF),
            pltpu.VMEM((DS, 256), BF),
            pltpu.VMEM((3, DS, 512), BF),
            pltpu.VMEM((3, DS, 512), BF),
            pltpu.VMEM((DS, 256), BF),
            pltpu.VMEM((DS, 256), BF),
            pltpu.VMEM((4, 8 * TOK, 512), F32),
            pltpu.VMEM((8 * TOK, 256), F32),
            pltpu.VMEM((4, 2, TOK, 256), BF),
            pltpu.VMEM((4, 2, TOK, 256), BF),
            pltpu.VMEM((4, 3, 2, TOK, 512), BF),
            pltpu.VMEM((4, 3, 2, TOK, 512), BF),
            pltpu.VMEM((2, TOK, 128), BF),
            pltpu.VMEM((2, TOK, 128), BF),
            pltpu.VMEM((3, 2, TOK, 256), BF),
            pltpu.VMEM((3, 2, TOK, 256), BF),
            pltpu.VMEM((TOK, 256), F32),
            pltpu.VMEM((TOK, 256), BF),
            pltpu.VMEM((TOK, 256), BF),
            pltpu.VMEM((8 * TOK, 128), F32),
            pltpu.VMEM((4, 2, TOK, 128), BF),
            pltpu.VMEM((4, 2, TOK, 128), BF),
            pltpu.VMEM((2 * R, DS), F32),
            pltpu.VMEM((2 * R, R), F32),
            pltpu.VMEM((2 * R, DS), F32),
            pltpu.VMEM((2 * R, R), F32),
            pltpu.VMEM((128, GR), F32),
            pltpu.VMEM((GP, 128), F32),
            pltpu.VMEM((GP, 128), F32),
            pltpu.VMEM((GH + 32, 128), BF),
            pltpu.VMEM((GH + 32, 128), BF),
            pltpu.VMEM((GH, 128), BF),
            pltpu.VMEM((NZ, GZ, 128), BF),
            pltpu.VMEM((GZ, 128), F32),
            pltpu.VMEM((3, GZ, 128), F32),
            pltpu.VMEM((2, NZ, 2, GZ, 128), BF),
            pltpu.VMEM((2, NY, 2, 32, 128), BF),
            pltpu.VMEM((NY, 32, 128), BF),
            pltpu.VMEM((NZ, 32, 128), BF),
            pltpu.VMEM((32, 128), F32),
            pltpu.VMEM((3, 32, 128), F32),
            pltpu.VMEM((ROWS, STEPS, QH * HD), BF),
            pltpu.VMEM((QH, TOK, HD), F32),
            pltpu.VMEM((KVH, 256, HD), BF),
            pltpu.VMEM((256, 1024), BF),
            pltpu.VMEM((256, 1024), BF),
            pltpu.VMEM((256, 256), F32),
            pltpu.VMEM((TOK, 256), F32),
            pltpu.VMEM((TOK, HD), F32),
            pltpu.VMEM((TOK, HD), F32),
            pltpu.VMEM((KVH, 1, 256), F32),
            pltpu.VMEM((KVH, 1, 256), F32),
            pltpu.VMEM((KVH, HD, 256), F32),
            pltpu.VMEM((KVH, TOK, 256), BF),
            pltpu.VMEM((QH, TOK, HD), F32),
            pltpu.VMEM((ROWS, STEPS, QH * HD), BF),
            pltpu.VMEM((2 * R, DS), F32),
            pltpu.VMEM((2 * R, R), F32),
            pltpu.SemaphoreType.DMA((N_LOCAL,)),
            pltpu.SemaphoreType.DMA((N_REMOTE,)),
            pltpu.SemaphoreType.DMA((N_REMOTE,)),
        ],
        compiler_params=pltpu.CompilerParams(
            collective_id=0, has_side_effects=True, vmem_limit_bytes=56 * 1024 * 1024
        ),
    )(*operands)


def results_kernel(att, na, nb, att_out, na_out, nb_out, attv, nav, nbv, sem):
    parts = [(att.at[pl.ds(3 * i, 3)], attv.at[pl.ds(3 * i, 3)], att_out.at[pl.ds(3 * i, 3)])
             for i in range(5)]
    parts += [(na, nav, na_out), (nb, nbv, nb_out)]
    reads = [pltpu.make_async_copy(x, v, sem.at[0, i]) for i, (x, v, _) in enumerate(parts)]
    writes = [pltpu.make_async_copy(v, o, sem.at[1, i]) for i, (_, v, o) in enumerate(parts)]
    for cp in reads:
        cp.start()
    for read, write in zip(reads, writes):
        read.wait()
        write.start()
    for cp in writes:
        cp.wait()


def results(*operands):
    hbm = pl.BlockSpec(memory_space=pltpu.HBM)
    return pl.pallas_call(
        results_kernel,
        out_shape=tuple(jax.ShapeDtypeStruct(x.shape, x.dtype) for x in operands),
        in_specs=[hbm] * 3,
        out_specs=(hbm,) * 3,
        scratch_shapes=[pltpu.VMEM(x.shape, x.dtype) for x in operands]
        + [pltpu.SemaphoreType.DMA((2, 7))],
        compiler_params=pltpu.CompilerParams(vmem_limit_bytes=56 * 1024 * 1024),
    )(*operands)


def per_device(
    hidden_in, kv_weight, factor_a, factor_b, grad_a, grad_b, key_gain,
    queries, cache_keys, cache_values, cache_lengths, positions,
):
    groups_dp = lax.axis_size("dp")
    rate_a = 2.0 / math.sqrt(groups_dp * D)
    rate_b = 2.0 / math.sqrt(groups_dp * R)
    attended, na, nb = results(*transfers(
        rate_a, rate_b, hidden_in.transpose(1, 2, 0), kv_weight,
        grad_a.reshape(2 * R, DS), grad_b.reshape(2 * R, R),
        factor_a.reshape(2 * R, DS), factor_b.reshape(2 * R, R),
        key_gain.reshape(1, HD), queries,
        cache_keys.reshape(16 * ROWS, KVH * HD), cache_values.reshape(16 * ROWS, KVH * HD),
        cache_lengths, positions,
    ))
    return (attended, na.reshape(2, R, DS), nb.reshape(2, R, R))


def solution(mesh):
    return jax.shard_map(
        per_device,
        mesh=mesh,
        in_specs=(
            P("dp", None, "tensor"),
            P(None, "tensor", None),
            P(None, None, "tensor"),
            P(None, None, "tensor"),
            P("dp", None, None, "tensor"),
            P("dp", None, None, "tensor"),
            P(),
            P(("dp", "tensor"), None, None),
            P(("dp", "tensor"), None, None),
            P(("dp", "tensor"), None, None),
            P(("dp", "tensor")),
            P(("dp", "tensor")),
        ),
        out_specs=(
            P(("dp", "tensor"), None, None),
            P(None, None, "tensor"),
            P(None, None, "tensor"),
        ),
        check_vma=False,
    )
```
